512 devices in a mesh: pair: 128 (over z, y, core), blk: 4 (over x).
Axes of the slice: x: 4, y: 8, z: 8, core: 2. Of those that a mesh axis runs over, the one named last changes fastest.
Arguments:
- amplitudes: bfloat16 [512, 102400], P(('pair', 'blk')), may hold values from -6 to 6
- integrals: bfloat16 [102400, 3200], P('pair', 'blk'), may hold values from -0.02734375 to 0.02734375
- residual_in: bfloat16 [512, 3200], P(('pair', 'blk')), may hold values from -6 to 6
- pair_irrep: int32 [512], P(('pair', 'blk')), may hold values from 0 to 7, as said below
- slab_irrep: int32 [128], replicated, may hold values from 0 to 7, as said below
- upper_irrep: int32 [4], replicated, may hold values from 0 to 7, as said below
- virt_irrep: int32 [800], replicated, may hold values from 0 to 7, as said below
Outputs:
- residual_out: bfloat16 [512, 3200], P(('pair', 'blk'))
The draws below stay inside these ranges and needn't reach their ends.
Inputs may be any that keep to these rules, and one draw needn't show every extreme that they name: `pair_irrep`: D2h irrep label of each occupied pair. `slab_irrep`: D2h irrep label of each lower slab orbital. `upper_irrep`: D2h irrep label of each upper slab orbital. `virt_irrep`: D2h irrep label of each virtual orbital.
All inputs are finite; a program needn't handle non-finite values.
Results may differ from the reference program's by a relative error of at most 0.00105.
Values may be sent and summed in bfloat16 or wider, within the bound.
No kernel may reach another device: no remote copies, remote signals or barrier semaphores. Data moves between devices by JAX's collectives and lax.ppermute only.
A program may use at most 64 MiB of HBM per device.

```python
import jax
import jax.numpy as jnp
from jax import lax

NV = 800
IRREPS = 8
C_DEV = 1
P_SIZE = 512
C = 128
A = 4
N_PAIR = 128


def shared_centers(key):
    slab_center = jax.random.randint(jax.random.fold_in(key, 101), (), 0, IRREPS)
    virt_center = jax.random.randint(jax.random.fold_in(key, 102), (), 0, IRREPS)
    return (slab_center.astype(jnp.int32), virt_center.astype(jnp.int32))


def skewed_labels(key, entries, center):
    choose_key, spread_key, place_key = jax.random.split(key, 3)
    chooser = jax.random.randint(choose_key, (entries,), 0, 4)
    spread_label = jax.random.randint(spread_key, (entries,), 0, IRREPS)
    labels = jnp.where(chooser < 3, center, spread_label).astype(jnp.int32)
    placing = jax.random.permutation(place_key, entries)
    labels = jnp.where(placing == 0, 0, labels)
    labels = jnp.where(placing == 1, IRREPS - 1, labels)
    return labels.astype(jnp.int32)


def draw_pair_irrep(key, part):
    slab_center, virt_center = shared_centers(key)
    key = jax.random.fold_in(key, 1)
    return skewed_labels(key, P_SIZE, jnp.bitwise_xor(slab_center, virt_center))


def draw_slab_irrep(key, part):
    slab_center, virt_center = shared_centers(key)
    key = jax.random.fold_in(key, 2)
    return skewed_labels(key, C, slab_center)


def draw_upper_irrep(key, part):
    slab_center, virt_center = shared_centers(key)
    key = jax.random.fold_in(key, 3)
    return skewed_labels(key, A, slab_center)


def draw_virt_irrep(key, part):
    slab_center, virt_center = shared_centers(key)
    key = jax.random.fold_in(key, 4)
    return skewed_labels(key, NV, virt_center)


def block_scale(key, extent, shards, least, high):
    gain = 1.0
    for axis_at, blocks in shards:
        draws = jax.random.uniform(jax.random.fold_in(jax.random.fold_in(key, 6), axis_at), (blocks,), jnp.float32, least / len(shards), high / len(shards))
        gain = gain * jnp.repeat(jnp.exp(draws), extent[axis_at] // blocks).reshape((-1,) + (1,) * (len(extent) - 1 - axis_at))
    return gain


def gaussian(own_key, extent, width, bound, shards=(), kind=jnp.bfloat16):
    values = jax.random.normal(own_key, extent, jnp.float32) * width
    if len(shards) > 0:
        values = block_scale(own_key, extent, shards, -0.22, 0.18) * values
    return jnp.clip(values, min=-bound, max=bound).astype(kind)


def setup_inputs(seed: int = 0) -> dict:
    key_list = jax.random.split(jax.random.key(seed), 8)
    return {
        "amplitudes": gaussian(key_list[0], (P_SIZE, C * NV), 1.0, 6.0, ((0, 512),)),
        "integrals": gaussian(key_list[1], (C * NV, A * NV), (C * NV // 2) ** -0.5, 0.02734375, ((0, 128), (1, 4))),
        "residual_in": gaussian(key_list[2], (P_SIZE, A * NV), 1.0, 6.0, ((0, 512),)),
        "pair_irrep": draw_pair_irrep(jax.random.fold_in(key_list[7], 71), 0),
        "slab_irrep": draw_slab_irrep(jax.random.fold_in(key_list[7], 71), 0),
        "upper_irrep": draw_upper_irrep(jax.random.fold_in(key_list[7], 71), 0),
        "virt_irrep": draw_virt_irrep(jax.random.fold_in(key_list[7], 71), 0),
    }


def reference(amplitudes, integrals, residual_in, pair_irrep, slab_irrep, upper_irrep, virt_irrep):
    cd_irrep = jnp.bitwise_xor(slab_irrep[:, None], virt_irrep[None, :]).reshape(-1)
    ab_irrep = jnp.bitwise_xor(upper_irrep[:, None], virt_irrep[None, :]).reshape(-1)
    nothing = jnp.zeros((), amplitudes.dtype)
    kept_amp = jnp.where(pair_irrep[:, None] == cd_irrep[None, :], amplitudes, nothing)
    block_width = C_DEV * NV

    def accumulate(index, running_sum):
        offset_row = (index * block_width).astype(jnp.int32)
        amp_block = lax.dynamic_slice_in_dim(kept_amp, offset_row, block_width, 1)
        int_block = lax.dynamic_slice_in_dim(integrals, offset_row, block_width, 0)
        cd_block = lax.dynamic_slice_in_dim(cd_irrep, offset_row, block_width, 0)
        int_kept = jnp.where(cd_block[:, None] == ab_irrep[None, :], int_block, jnp.zeros((), integrals.dtype))
        return running_sum + jnp.dot(amp_block, int_kept, preferred_element_type=jnp.float32)

    ladder = lax.fori_loop(0, N_PAIR, accumulate, jnp.zeros((P_SIZE, A * NV), jnp.float32))
    return (residual_in.astype(jnp.float32) + ladder).astype(jnp.bfloat16)
```

```python
import jax
import jax.numpy as jnp
from jax import lax
from jax.sharding import Mesh
from jax.sharding import PartitionSpec as P

AXES = ("z", "y", "core", "x1", "x0")
SCALE = 64.0


def per_device(amplitudes, integrals, residual_in, pair_irrep, slab_irrep, upper_irrep, virt_irrep):
    bf16, f32, f16 = jnp.bfloat16, jnp.float32, jnp.float16
    nv = virt_irrep.shape[0]
    core = lax.axis_index("core")
    x1 = lax.axis_index("x1")
    x0 = lax.axis_index("x0")
    x = 2 * x1 + x0
    slab = lax.axis_index(("z", "y", "core"))
    zy = lax.axis_size("z") * lax.axis_size("y")

    partner_v = lax.ppermute(integrals, ("x1", "x0"), [(0, 3), (3, 0), (1, 2), (2, 1)])

    chunks = amplitudes.reshape(zy, 2, nv).swapaxes(0, 1).reshape(2 * zy, nv)
    mine = lax.all_to_all(chunks, ("core", "z", "y"), 0, 0, tiled=True)
    other = lax.ppermute(mine, "x0", [(0, 1), (1, 0)])

    rows = jnp.stack([mine, other]).reshape(2, 2, zy, nv)
    keep_rows = lax.dynamic_index_in_dim(rows, core, 1, keepdims=False).reshape(2 * zy, nv)
    send_rows = lax.dynamic_index_in_dim(rows, 1 - core, 1, keepdims=False).reshape(2 * zy, nv)

    cd_irrep = jnp.bitwise_xor(lax.dynamic_index_in_dim(slab_irrep, slab, 0), virt_irrep)
    zero = jnp.zeros((), bf16)

    def kept(block, a):
        ab = jnp.bitwise_xor(lax.dynamic_index_in_dim(upper_irrep, a, 0), virt_irrep)
        return jnp.where(cd_irrep[:, None] == ab[None, :], block, zero)

    v = jnp.concatenate([kept(integrals, x), kept(partner_v, 3 - x)], axis=1)
    send = jnp.dot(send_rows, v, preferred_element_type=f32)
    got = lax.ppermute(send, "core", [(0, 1), (1, 0)])
    keep = jnp.dot(keep_rows, v, preferred_element_type=f32)
    part = ((keep + got) * SCALE).astype(f16).reshape(2, zy, 2 * nv)
    part = jnp.where(x0 == 0, part, part[::-1])
    back = lax.all_to_all(part.reshape(2 * zy, 2 * nv), ("x0", "z", "y"), 0, 0, tiled=True)
    sums = jnp.sum(back.reshape(2, zy, 2, nv).astype(f32), axis=1) * (1.0 / SCALE)
    order = jnp.stack([sums[0, 0], sums[1, 0], sums[1, 1], sums[0, 1]])
    ladder = jnp.where(x1 == 0, order, jnp.roll(order, 2, axis=0))
    ab_irrep = jnp.bitwise_xor(upper_irrep[:, None], virt_irrep[None, :])
    ladder = jnp.where(ab_irrep == pair_irrep[0], ladder, 0.0).reshape(1, -1)
    return (residual_in.astype(f32) + ladder).astype(bf16)


def solution(mesh):
    fine = Mesh(mesh.devices.reshape(8, 8, 2, 2, 2), AXES)
    return jax.shard_map(
        per_device,
        mesh=fine,
        in_specs=(P(AXES, None), P(AXES[:3], AXES[3:]), P(AXES, None), P(AXES), P(), P(), P()),
        out_specs=P(AXES, None),
        check_vma=False,
    )
```

```python
import functools

import jax
import jax.numpy as jnp
from jax import lax
from jax.experimental import pallas as pl
from jax.experimental.pallas import tpu as pltpu
from jax.sharding import Mesh
from jax.sharding import PartitionSpec as P

AXES = ("z", "y", "core", "x1", "x0")
BF16, F32, F16 = jnp.bfloat16, jnp.float32, jnp.float16
NV = 800
LANES = 128
TILES = 7
WIDE = TILES * LANES
SCALE = 64.0

VMEM = pl.BlockSpec(memory_space=pltpu.VMEM)
SMEM = pl.BlockSpec(memory_space=pltpu.SMEM)


def call(body, out, ins, flops, nbytes, scratch=()):
    return pl.pallas_call(
        body,
        out_shape=out,
        in_specs=[SMEM if kind == "s" else VMEM for kind in ins],
        out_specs=VMEM,
        scratch_shapes=list(scratch),
        compiler_params=pltpu.CompilerParams(vmem_limit_bytes=32 * 1024 * 1024),
        cost_estimate=pl.CostEstimate(flops=flops, bytes_accessed=nbytes, transcendentals=0),
    )


def cut_body(row_ref, out_ref):
    filler = jnp.zeros((1, LANES), F32)

    def four(q, carry):
        for r in range(4):
            at = [pl.multiple_of(q * 3200 + (6 * r + t) * LANES, LANES) for t in range(TILES)]
            tiles = [row_ref[:, pl.ds(a, LANES)].astype(F32) for a in at]
            out_ref[r % 2, 2 * q + r // 2] = jnp.concatenate(tiles + [filler], axis=0).astype(BF16)
        return carry

    lax.fori_loop(0, 32, four, 0, unroll=4)


def kept_body(scalars_ref, virt_ref, block_ref, out_ref):
    slab, upper, shift = scalars_ref[0], scalars_ref[1], scalars_ref[2]
    label = lax.broadcasted_iota(jnp.int32, (16, NV), 0)
    virt = virt_ref[...]
    rows = jnp.where(label == jnp.bitwise_xor(virt, slab), 1.0, 0.0).astype(BF16)
    columns = jnp.where(label == jnp.bitwise_xor(virt, upper), 1.0, 0.0).astype(BF16)
    same = lax.dot_general(rows, columns, (((0,), (0,)), ((), ())), preferred_element_type=F32)
    out_ref[...] = jnp.zeros_like(out_ref)
    kept = jnp.where(same > 0.5, block_ref[...].astype(F32), 0.0).astype(BF16)
    out_ref[pl.ds(pl.multiple_of(shift, 32), NV), 0:NV] = kept


def ladder_body(flip, zy, scalars_ref, mine_ref, other_ref, own_ref, partner_ref, out_ref, rows, lhs):
    core, x0 = scalars_ref[0], scalars_ref[1]
    pick = 1 - core if flip else core
    first = pl.multiple_of(pick * (zy * 8), zy * 8)
    for block, source in ((0, mine_ref), (1, other_ref)):
        rows[...] = source[pl.ds(first, zy * 8), :].astype(F32)
        place = x0 if block == 0 else 1 - x0
        for t in range(TILES):
            lhs[pl.ds(pl.multiple_of(place * zy, zy), zy), t * LANES : (t + 1) * LANES] = rows[
                pl.ds(t, zy, stride=8), :
            ].astype(BF16)
    for half, v_ref in ((0, own_ref), (1, partner_ref)):
        sums = jnp.dot(lhs[...], v_ref[...], preferred_element_type=F32)
        for t in range(TILES):
            out_ref[pl.ds(8 * half + t, 2 * zy, stride=16), :] = sums[:, t * LANES : (t + 1) * LANES]
        out_ref[pl.ds(8 * half + TILES, 2 * zy, stride=16), :] = jnp.zeros((2 * zy, LANES), F32)


def finish_body(scalars_ref, sums_ref, virt_ref, old_ref, out_ref):
    swap = scalars_ref[0] == 1
    pair = scalars_ref[1]
    order = ((0, 0), (1, 0), (1, 1), (0, 1))
    virt = virt_ref[...]
    for a in range(4):
        s, h = order[a]
        s2, h2 = order[(a + 2) % 4]
        straight = sums_ref[s, 8 * h : 8 * h + 8, :]
        turned = sums_ref[s2, 8 * h2 : 8 * h2 + 8, :]
        tiles = jnp.where(swap, turned, straight) * (1.0 / SCALE)
        row = jnp.concatenate([tiles[t : t + 1, :] for t in range(TILES)], axis=1)[:, :NV]
        ab = jnp.bitwise_xor(virt, scalars_ref[2 + a])
        row = jnp.where(ab == pair, row, 0.0)
        old = old_ref[:, a * NV : (a + 1) * NV].astype(F32)
        out_ref[:, a * NV : (a + 1) * NV] = (old + row).astype(BF16)


def per_device(amplitudes, integrals, residual_in, pair_irrep, slab_irrep, upper_irrep, virt_irrep):
    core = lax.axis_index("core")
    x1 = lax.axis_index("x1")
    x0 = lax.axis_index("x0")
    x = 2 * x1 + x0
    slab = lax.axis_index(("z", "y", "core"))
    zy = lax.axis_size("z") * lax.axis_size("y")
    shape = jax.ShapeDtypeStruct
    virt = virt_irrep.reshape(1, NV)

    partner = lax.ppermute(integrals, ("x1", "x0"), [(0, 3), (3, 0), (1, 2), (2, 1)])

    cut = call(cut_body, shape((2, zy, 8, LANES), BF16), "v", 0, 700000)(amplitudes)
    mine = lax.all_to_all(cut.reshape(2 * zy, 8, LANES), ("core", "z", "y"), 0, 0, tiled=True)
    mine = mine.reshape(2 * zy * 8, LANES)
    other = lax.ppermute(mine, "x0", [(0, 1), (1, 0)])

    slab_label = lax.dynamic_index_in_dim(slab_irrep, slab, 0, keepdims=False)
    shift = 32 * (slab % 4)

    def kept(block, a):
        upper = lax.dynamic_index_in_dim(upper_irrep, a, 0, keepdims=False)
        scalars = jnp.stack([slab_label, upper, shift])
        return call(kept_body, shape((WIDE, WIDE), BF16), "svv", 20000000, 3000000)(scalars, virt, block)

    own_v = kept(integrals, x)
    partner_v = kept(partner, 3 - x)

    places = jnp.stack([core, x0])

    def ladder(flip):
        return call(
            functools.partial(ladder_body, flip, zy),
            shape((2 * zy * 16, LANES), F32),
            "svvvv",
            2 * 128 * 1792 * 896,
            5000000,
            [pltpu.VMEM((zy * 8, LANES), F32), pltpu.VMEM((2 * zy, WIDE), BF16)],
        )(places, mine, other, own_v, partner_v)

    got = lax.ppermute(ladder(True), "core", [(0, 1), (1, 0)])
    keep = ladder(False)
    part = ((keep + got) * SCALE).astype(F16).reshape(2 * zy, 16, LANES)
    back = lax.all_to_all(part, ("x0", "z", "y"), 0, 0, tiled=True)
    sums = jnp.sum(back.reshape(2, zy, 16, LANES).astype(F32), axis=1)
    scalars = jnp.concatenate([jnp.stack([x1, pair_irrep[0]]), upper_irrep])
    return call(finish_body, shape((1, 4 * NV), BF16), "svvv", 0, 50000)(scalars, sums, virt, residual_in)


def solution(mesh):
    fine = Mesh(mesh.devices.reshape(8, 8, 2, 2, 2), AXES)
    return jax.shard_map(
        per_device,
        mesh=fine,
        in_specs=(P(AXES, None), P(AXES[:3], AXES[3:]), P(AXES, None), P(AXES), P(), P(), P()),
        out_specs=P(AXES, None),
        check_vma=False,
    )
```

```python
import functools

import jax
import jax.numpy as jnp
from jax import lax
from jax.experimental import pallas as pl
from jax.experimental.pallas import tpu as pltpu
from jax.sharding import Mesh
from jax.sharding import PartitionSpec as P

AXES = ("z", "y", "core", "x1", "x0")
BF16, F32, F16 = jnp.bfloat16, jnp.float32, jnp.float16
NV = 800
LANES = 128
TILES = 7
WIDE = TILES * LANES
SCALE = 64.0

VMEM = pl.BlockSpec(memory_space=pltpu.VMEM)
SMEM = pl.BlockSpec(memory_space=pltpu.SMEM)


def call(body, out, ins, flops, nbytes, scratch=()):
    return pl.pallas_call(
        body,
        out_shape=out,
        in_specs=[SMEM if kind == "s" else VMEM for kind in ins],
        out_specs=VMEM,
        scratch_shapes=list(scratch),
        compiler_params=pltpu.CompilerParams(vmem_limit_bytes=32 * 1024 * 1024),
        cost_estimate=pl.CostEstimate(flops=flops, bytes_accessed=nbytes, transcendentals=0),
    )


def cut_body(row_ref, out_ref):
    filler = jnp.zeros((1, LANES), F32)

    def four(q, carry):
        for r in range(4):
            at = [pl.multiple_of(q * 3200 + (6 * r + t) * LANES, LANES) for t in range(TILES)]
            tiles = [row_ref[:, pl.ds(a, LANES)].astype(F32) for a in at]
            out_ref[r % 2, 2 * q + r // 2] = jnp.concatenate(tiles + [filler], axis=0).astype(BF16)
        return carry

    lax.fori_loop(0, 32, four, 0, unroll=4)


def kept_body(partner, places_ref, slab_ref, upper_ref, virt_ref, block_ref, out_ref):
    x, c = 2 * places_ref[2] + places_ref[1], places_ref[3]
    slab, upper, shift = slab_ref[c], upper_ref[3 - x if partner else x], 32 * (c % 4)
    label = lax.broadcasted_iota(jnp.int32, (16, NV), 0)
    virt = virt_ref[...].reshape(1, NV)
    rows = jnp.where(label == jnp.bitwise_xor(virt, slab), 1.0, 0.0).astype(BF16)
    columns = jnp.where(label == jnp.bitwise_xor(virt, upper), 1.0, 0.0).astype(BF16)
    same = lax.dot_general(rows, columns, (((0,), (0,)), ((), ())), preferred_element_type=F32)
    out_ref[...] = jnp.zeros_like(out_ref)
    kept = jnp.where(same > 0.5, block_ref[...].astype(F32), 0.0).astype(BF16)
    out_ref[pl.ds(pl.multiple_of(shift, 32), NV), 0:NV] = kept


def ladder_body(flip, zy, scalars_ref, mine_ref, other_ref, own_ref, partner_ref, out_ref, rows, lhs):
    core, x0 = scalars_ref[0], scalars_ref[1]
    pick = 1 - core if flip else core
    first = pl.multiple_of(pick * (zy * 8), zy * 8)
    for block, source in ((0, mine_ref), (1, other_ref)):
        rows[...] = source[pl.ds(first, zy * 8), :].astype(F32)
        place = x0 if block == 0 else 1 - x0
        for t in range(TILES):
            lhs[pl.ds(pl.multiple_of(place * zy, zy), zy), t * LANES : (t + 1) * LANES] = rows[
                pl.ds(t, zy, stride=8), :
            ].astype(BF16)
    for half, v_ref in ((0, own_ref), (1, partner_ref)):
        sums = jnp.dot(lhs[...], v_ref[...], preferred_element_type=F32)
        for t in range(TILES):
            out_ref[pl.ds(8 * half + t, 2 * zy, stride=16), :] = sums[:, t * LANES : (t + 1) * LANES]
        out_ref[pl.ds(8 * half + TILES, 2 * zy, stride=16), :] = jnp.zeros((2 * zy, LANES), F32)


def finish_body(places_ref, pair_ref, upper_ref, sums_ref, virt_ref, old_ref, out_ref):
    swap = places_ref[2] == 1
    pair = pair_ref[0]
    order = ((0, 0), (1, 0), (1, 1), (0, 1))
    virt = virt_ref[...].reshape(1, NV)
    for a in range(4):
        s, h = order[a]
        s2, h2 = order[(a + 2) % 4]
        straight = sums_ref[s, 8 * h : 8 * h + 8, :]
        turned = sums_ref[s2, 8 * h2 : 8 * h2 + 8, :]
        tiles = jnp.where(swap, turned, straight) * (1.0 / SCALE)
        row = jnp.concatenate([tiles[t : t + 1, :] for t in range(TILES)], axis=1)[:, :NV]
        ab = jnp.bitwise_xor(virt, upper_ref[a])
        row = jnp.where(ab == pair, row, 0.0)
        old = old_ref[:, a * NV : (a + 1) * NV].astype(F32)
        out_ref[:, a * NV : (a + 1) * NV] = (old + row).astype(BF16)


def per_device(amplitudes, integrals, residual_in, pair_irrep, slab_irrep, upper_irrep, virt_irrep):
    core = lax.axis_index("core")
    x1 = lax.axis_index("x1")
    x0 = lax.axis_index("x0")
    slab = lax.axis_index(("z", "y", "core"))
    zy = lax.axis_size("z") * lax.axis_size("y")
    shape = jax.ShapeDtypeStruct
    places = jnp.stack([core, x0, x1, slab])

    partner = lax.ppermute(integrals, ("x1", "x0"), [(0, 3), (3, 0), (1, 2), (2, 1)])

    cut = call(cut_body, shape((2, zy, 8, LANES), BF16), "v", 0, 700000)(amplitudes)
    mine = lax.all_to_all(cut.reshape(2 * zy, 8, LANES), ("core", "z", "y"), 0, 0, tiled=True)
    mine = mine.reshape(2 * zy * 8, LANES)

    def kept(block, partner):
        body = functools.partial(kept_body, partner)
        fill = call(body, shape((WIDE, WIDE), BF16), "sssvv", 20000000, 3000000)
        return fill(places, slab_irrep, upper_irrep, virt_irrep, block)

    own_v, mine = lax.optimization_barrier((kept(integrals, False), mine))
    other = lax.ppermute(mine, "x0", [(0, 1), (1, 0)])
    partner_v = kept(partner, True)

    def ladder(flip):
        return call(
            functools.partial(ladder_body, flip, zy),
            shape((2 * zy * 16, LANES), F32),
            "svvvv",
            2 * 128 * 1792 * 896,
            5000000,
            [pltpu.VMEM((zy * 8, LANES), F32), pltpu.VMEM((2 * zy, WIDE), BF16)],
        )(places, mine, other, own_v, partner_v)

    got = lax.ppermute(ladder(True), "core", [(0, 1), (1, 0)])
    keep = ladder(False)
    part = ((keep + got) * SCALE).astype(F16).reshape(2 * zy, 16, LANES)
    back = lax.all_to_all(part, ("x0", "z", "y"), 0, 0, tiled=True)
    sums = jnp.sum(back.reshape(2, zy, 16, LANES).astype(F32), axis=1)
    finish = call(finish_body, shape((1, 4 * NV), BF16), "sssvvv", 0, 50000)
    return finish(places, pair_irrep, upper_irrep, sums, virt_irrep, residual_in)


def solution(mesh):
    fine = Mesh(mesh.devices.reshape(8, 8, 2, 2, 2), AXES)
    return jax.shard_map(
        per_device,
        mesh=fine,
        in_specs=(P(AXES, None), P(AXES[:3], AXES[3:]), P(AXES, None), P(AXES), P(), P(), P()),
        out_specs=P(AXES, None),
        check_vma=False,
    )
```

```python
import functools

import jax
import jax.numpy as jnp
from jax import lax
from jax.experimental import pallas as pl
from jax.experimental.pallas import tpu as pltpu
from jax.sharding import Mesh
from jax.sharding import PartitionSpec as P

AXES = ("z", "y", "core", "x1", "x0")
BF16, F32, F16 = jnp.bfloat16, jnp.float32, jnp.float16
NV = 800
LANES = 128
TILES = 7
WIDE = TILES * LANES
SCALE = 64.0

VMEM = pl.BlockSpec(memory_space=pltpu.VMEM)
SMEM = pl.BlockSpec(memory_space=pltpu.SMEM)


def call(body, out, ins, flops, nbytes, scratch=()):
    return pl.pallas_call(
        body,
        out_shape=out,
        in_specs=[SMEM if kind == "s" else VMEM for kind in ins],
        out_specs=jax.tree.map(lambda _: VMEM, out),
        scratch_shapes=list(scratch),
        compiler_params=pltpu.CompilerParams(vmem_limit_bytes=16 * 1024 * 1024),
        cost_estimate=pl.CostEstimate(flops=flops, bytes_accessed=nbytes, transcendentals=0),
    )


def cut_body(steps, row_ref, out_ref, row, cut, in_sems, out_sems):
    filler = jnp.zeros((1, LANES), F32)
    lanes, slabs = row.shape[1] // steps, cut.shape[1] // steps

    def fetch(i):
        part = pl.ds(i * lanes, lanes)
        return pltpu.make_async_copy(row_ref.at[:, part], row.at[:, part], in_sems.at[i])

    def put(i):
        part = pl.ds(i * slabs, slabs)
        return pltpu.make_async_copy(cut.at[:, part], out_ref.at[:, part], out_sems.at[i])

    def four(q, carry):
        for r in range(4):
            at = [pl.multiple_of(q * 3200 + (6 * r + t) * LANES, LANES) for t in range(TILES)]
            tiles = [row[:, pl.ds(a, LANES)].astype(F32) for a in at]
            cut[r % 2, 2 * q + r // 2] = jnp.concatenate(tiles + [filler], axis=0).astype(BF16)
        return carry

    for i in range(steps):
        fetch(i).start()
    for i in range(steps):
        fetch(i).wait()
        lax.fori_loop(i * slabs // 2, (i + 1) * slabs // 2, four, 0, unroll=4)
        put(i).start()
    for i in range(steps):
        put(i).wait()


def kept_body(places_ref, slab_ref, upper_ref, virt_ref, block_ref, own_ref, mask_ref):
    x, slab = 2 * places_ref[2] + places_ref[1], slab_ref[places_ref[3]]
    label = lax.broadcasted_iota(jnp.int32, (16, NV), 0)
    virt = virt_ref[...].reshape(1, NV)
    rows = jnp.where(label == jnp.bitwise_xor(virt, slab), 1.0, 0.0).astype(BF16)

    def same(a):
        columns = jnp.where(label == jnp.bitwise_xor(virt, upper_ref[a]), 1.0, 0.0).astype(BF16)
        return lax.dot_general(rows, columns, (((0,), (0,)), ((), ())), preferred_element_type=F32)

    own_ref[...] = jnp.where(same(x) > 0.5, block_ref[...].astype(F32), 0.0).astype(BF16)
    mask_ref[...] = same(3 - x).astype(BF16)


def put_tiles(sums, count, out_ref, first, step):
    wide = jnp.concatenate([sums, jnp.zeros((count, WIDE - NV), F32)], axis=1)
    for t in range(TILES):
        out_ref[pl.ds(first + t, count, stride=step), :] = wide[:, t * LANES : (t + 1) * LANES]
    out_ref[pl.ds(first + TILES, count, stride=step), :] = jnp.zeros((count, LANES), F32)


def rows_body(zy, places_ref, mine_ref, other_ref, own_ref, lhs_ref, out_ref, wide):
    x0, r = places_ref[1], places_ref[3] % 4
    for block, source in ((0, mine_ref), (1, other_ref)):
        place = pl.multiple_of((x0 if block == 0 else 1 - x0) * zy, zy)
        out_ref[0 : zy * 8, :] = source[...].astype(F32)
        for t in range(TILES):
            wide[pl.ds(place, zy), t * LANES : (t + 1) * LANES] = out_ref[pl.ds(t, zy, stride=8), :]
    for shift in range(4):

        @pl.when(r == shift)
        def _():
            lhs_ref[...] = wide[:, 32 * shift : 32 * shift + NV].astype(BF16)

    sums = jnp.dot(lhs_ref[...], own_ref[...], preferred_element_type=F32)
    put_tiles(sums, 2 * zy, out_ref, 0, 8)


def ladder_body(zy, lhs_ref, own_sums_ref, partner_ref, mask_ref, out_ref):
    kept = partner_ref[...] * mask_ref[...]
    sums = jnp.dot(lhs_ref[...], kept, preferred_element_type=F32)
    put_tiles(sums, 2 * zy, out_ref, 8, 16)
    for t in range(8):
        out_ref[pl.ds(t, 2 * zy, stride=16), :] = own_sums_ref[pl.ds(t, 2 * zy, stride=8), :]


def finish_body(places_ref, pair_ref, upper_ref, sums_ref, virt_ref, old_ref, out_ref):
    swap = places_ref[2] == 1
    pair = pair_ref[0]
    order = ((0, 0), (1, 0), (1, 1), (0, 1))
    virt = virt_ref[...].reshape(1, NV)
    for a in range(4):
        s, h = order[a]
        s2, h2 = order[(a + 2) % 4]
        straight = sums_ref[s, 8 * h : 8 * h + 8, :]
        turned = sums_ref[s2, 8 * h2 : 8 * h2 + 8, :]
        tiles = jnp.where(swap, turned, straight) * (1.0 / SCALE)
        row = jnp.concatenate([tiles[t : t + 1, :] for t in range(TILES)], axis=1)[:, :NV]
        ab = jnp.bitwise_xor(virt, upper_ref[a])
        row = jnp.where(ab == pair, row, 0.0)
        old = old_ref[:, a * NV : (a + 1) * NV].astype(F32)
        out_ref[:, a * NV : (a + 1) * NV] = (old + row).astype(BF16)


def per_device(amplitudes, integrals, residual_in, pair_irrep, slab_irrep, upper_irrep, virt_irrep):
    core = lax.axis_index("core")
    x1 = lax.axis_index("x1")
    x0 = lax.axis_index("x0")
    slab = lax.axis_index(("z", "y", "core"))
    zy = lax.axis_size("z") * lax.axis_size("y")
    shape = jax.ShapeDtypeStruct
    places = jnp.stack([core, x0, x1, slab])

    partner = lax.ppermute(integrals, ("x1", "x0"), [(0, 3), (3, 0), (1, 2), (2, 1)])

    steps = 4
    cut = pl.pallas_call(
        functools.partial(cut_body, steps),
        in_specs=[pl.BlockSpec(memory_space=pl.ANY)],
        out_specs=pl.BlockSpec(memory_space=pl.ANY),
        out_shape=shape((2, zy, 8, LANES), BF16),
        scratch_shapes=[
            pltpu.VMEM(amplitudes.shape, BF16),
            pltpu.VMEM((2, zy, 8, LANES), BF16),
            pltpu.SemaphoreType.DMA((steps,)),
            pltpu.SemaphoreType.DMA((steps,)),
        ],
        cost_estimate=pl.CostEstimate(flops=0, bytes_accessed=700000, transcendentals=0),
    )(amplitudes)
    mine = lax.all_to_all(cut.reshape(2 * zy, 8, LANES), ("core", "z", "y"), 0, 0, tiled=True)
    mine = mine.reshape(2 * zy * 8, LANES)

    fill = call(kept_body, [shape((NV, NV), BF16)] * 2, "sssvv", 20000000, 3000000)
    own_v, mask = fill(places, slab_irrep, upper_irrep, virt_irrep, integrals)
    own_v, mask, mine = lax.optimization_barrier((own_v, mask, mine))
    half, tiles = shape((2 * zy, NV), BF16), shape((2 * zy * 8, LANES), F32)
    rows = call(
        functools.partial(rows_body, zy),
        [half, tiles],
        "svvv",
        2 * 128 * 800 * 800,
        3000000,
        [pltpu.VMEM((2 * zy, WIDE), F32)],
    )
    ladder = call(
        functools.partial(ladder_body, zy),
        shape((2 * zy * 16, LANES), F32),
        "vvvv",
        2 * 128 * 800 * 800,
        5000000,
    )

    def exchanged(of_core):
        here = lax.dynamic_slice_in_dim(mine, of_core * (zy * 8), zy * 8, 0)
        return here, lax.ppermute(here, "x0", [(0, 1), (1, 0)])

    send_rows, keep_rows = exchanged(1 - core), exchanged(core)
    send = ladder(*rows(places, *send_rows, own_v), partner, mask)
    send, keep_rows = lax.optimization_barrier((send, keep_rows))
    got = lax.ppermute(send, "core", [(0, 1), (1, 0)])
    keep = ladder(*rows(places, *keep_rows, own_v), partner, mask)
    part = ((keep + got) * SCALE).astype(F16).reshape(2 * zy, 16, LANES)
    back = lax.all_to_all(part, ("x0", "z", "y"), 0, 0, tiled=True)
    sums = jnp.sum(back.reshape(2, zy, 16, LANES).astype(F32), axis=1)
    finish = call(finish_body, shape((1, 4 * NV), BF16), "sssvvv", 0, 50000)
    return finish(places, pair_irrep, upper_irrep, sums, virt_irrep, residual_in)


def solution(mesh):
    fine = Mesh(mesh.devices.reshape(8, 8, 2, 2, 2), AXES)
    return jax.shard_map(
        per_device,
        mesh=fine,
        in_specs=(P(AXES, None), P(AXES[:3], AXES[3:]), P(AXES, None), P(AXES), P(), P(), P()),
        out_specs=P(AXES, None),
        check_vma=False,
    )
```

```python
import functools

import jax
import jax.numpy as jnp
from jax import lax
from jax.experimental import pallas as pl
from jax.experimental.pallas import tpu as pltpu
from jax.sharding import Mesh
from jax.sharding import PartitionSpec as P

AXES = ("z", "y", "core", "x1", "x0")
BF16, F32, F16 = jnp.bfloat16, jnp.float32, jnp.float16
NV = 800
LANES = 128
TILES = 7
WIDE = TILES * LANES
SCALE = 64.0

VMEM = pl.BlockSpec(memory_space=pltpu.VMEM)
SMEM = pl.BlockSpec(memory_space=pltpu.SMEM)


def call(body, out, ins, flops, nbytes, scratch=()):
    return pl.pallas_call(
        body,
        out_shape=out,
        in_specs=[SMEM if kind == "s" else VMEM for kind in ins],
        out_specs=jax.tree.map(lambda _: VMEM, out),
        scratch_shapes=list(scratch),
        compiler_params=pltpu.CompilerParams(vmem_limit_bytes=16 * 1024 * 1024),
        cost_estimate=pl.CostEstimate(flops=flops, bytes_accessed=nbytes, transcendentals=0),
    )


def cut_body(steps, pair_ref, row_ref, out_ref, pair, row, cut, pair_sem, in_sems, out_sems):
    lanes, slabs = row.shape[1] // steps, cut.shape[0] // steps

    def fetch(i):
        part = pl.ds(i * lanes, lanes)
        return pltpu.make_async_copy(row_ref.at[:, part], row.at[:, part], in_sems.at[i])

    def put(i):
        part = pl.ds(i * slabs, slabs)
        return pltpu.make_async_copy(cut.at[part], out_ref.at[part], out_sems.at[i])

    label = pltpu.make_async_copy(pair_ref, pair, pair_sem)
    label.start()

    def four(q, carry):
        for r in range(4):
            at = [pl.multiple_of(q * 3200 + (6 * r + t) * LANES, LANES) for t in range(TILES)]
            tiles = [row[:, pl.ds(a, LANES)].astype(F32) for a in at]
            cut[4 * q + r] = jnp.concatenate(tiles + [filler], axis=0).astype(BF16)
        return carry

    for i in range(steps):
        fetch(i).start()
    label.wait()
    filler = jnp.full((1, LANES), pair[0].astype(F32))
    for i in range(steps):
        fetch(i).wait()
        lax.fori_loop(i * slabs // 4, (i + 1) * slabs // 4, four, 0, unroll=4)
        put(i).start()
    for i in range(steps):
        put(i).wait()


def put_tiles(sums, count, out_ref, first, step):
    wide = jnp.concatenate([sums, jnp.zeros((count, WIDE - NV), F32)], axis=1)
    for t in range(TILES):
        out_ref[pl.ds(first + t, count, stride=step), :] = wide[:, t * LANES : (t + 1) * LANES]
    out_ref[pl.ds(first + TILES, count, stride=step), :] = jnp.zeros((count, LANES), F32)


def kept_rows(flip, zy, places_ref, slab_ref, virt_ref, tiles_ref, flat, wide, lhs_ref, first):
    c = jnp.bitwise_xor(places_ref[3], flip)
    flat[...] = tiles_ref[:, jnp.bitwise_xor(places_ref[0], flip)].astype(F32).reshape(zy * 8, LANES)
    for t in range(TILES):
        wide[:, t * LANES : (t + 1) * LANES] = flat[pl.ds(t, zy, stride=8), :]
    pair = flat[pl.ds(TILES, zy, stride=8), :][:, 0:1]
    cd = jnp.bitwise_xor(virt_ref[...].reshape(1, NV), slab_ref[c]).astype(F32)
    for shift in range(4):

        @pl.when(c % 4 == shift)
        def _():
            row = wide[:, 32 * shift : 32 * shift + NV]
            lhs_ref[pl.ds(first, zy), :] = jnp.where(pair == cd, row, 0.0).astype(BF16)


def rows_body(zy, places_ref, slab_ref, virt_ref, tiles_ref, own_ref, lhs_ref, out_ref, flat, wide):
    kept_rows(0, zy, places_ref, slab_ref, virt_ref, tiles_ref, flat, wide, lhs_ref, 0)
    out_ref[...] = jnp.dot(lhs_ref[...], own_ref[...], preferred_element_type=F32)


def ordered(zy, places_ref, mine, there, rows):
    place = pl.multiple_of(places_ref[1] * zy, zy)
    rows[pl.ds(place, zy), :] = mine
    rows[pl.ds(pl.multiple_of(zy - place, zy), zy), :] = there


def other_body(zy, *refs):
    places_ref, slab_ref, virt_ref, mine_ref, there_ref, own_ref, sums_ref, sums2_ref = refs[:8]
    lhs_ref, out_ref, flat, wide, own_sums = refs[8:]
    place = pl.multiple_of(places_ref[1] * zy, zy)
    kept_rows(1, zy, places_ref, slab_ref, virt_ref, mine_ref, flat, wide, lhs_ref, place)
    there = pl.multiple_of(zy - place, zy)
    kept_rows(1, zy, places_ref, slab_ref, virt_ref, there_ref, flat, wide, lhs_ref, there)
    ordered(zy, places_ref, sums_ref[...], sums2_ref[...], own_sums)
    sums = own_sums[...] + jnp.dot(lhs_ref[...], own_ref[...], preferred_element_type=F32)
    put_tiles(sums, 2 * zy, out_ref, 0, 8)


def partner_body(zy, places_ref, mine_ref, there_ref, block_ref, out_ref, rows):
    ordered(zy, places_ref, mine_ref[...], there_ref[...], rows)
    out_ref[...] = jnp.dot(rows[...], block_ref[...], preferred_element_type=F32)


def ladder_body(zy, lhs_ref, block_ref, sums_ref, own_ref, out_ref):
    sums = sums_ref[...] + jnp.dot(lhs_ref[...], block_ref[...], preferred_element_type=F32)
    put_tiles(sums, 2 * zy, out_ref, 8, 16)
    for t in range(8):
        out_ref[pl.ds(t, 2 * zy, stride=16), :] = own_ref[pl.ds(t, 2 * zy, stride=8), :]


def finish_body(places_ref, pair_ref, upper_ref, sums_ref, virt_ref, old_ref, out_ref):
    swap = places_ref[2] == 1
    pair = pair_ref[0]
    order = ((0, 0), (1, 0), (1, 1), (0, 1))
    virt = virt_ref[...].reshape(1, NV)
    for a in range(4):
        s, h = order[a]
        s2, h2 = order[(a + 2) % 4]
        straight = sums_ref[s, 8 * h : 8 * h + 8, :]
        turned = sums_ref[s2, 8 * h2 : 8 * h2 + 8, :]
        tiles = jnp.where(swap, turned, straight) * (1.0 / SCALE)
        row = jnp.concatenate([tiles[t : t + 1, :] for t in range(TILES)], axis=1)[:, :NV]
        ab = jnp.bitwise_xor(virt, upper_ref[a])
        row = jnp.where(ab == pair, row, 0.0)
        old = old_ref[:, a * NV : (a + 1) * NV].astype(F32)
        out_ref[:, a * NV : (a + 1) * NV] = (old + row).astype(BF16)


def per_device(amplitudes, integrals, residual_in, pair_irrep, slab_irrep, upper_irrep, virt_irrep):
    core = lax.axis_index("core")
    x1 = lax.axis_index("x1")
    x0 = lax.axis_index("x0")
    slab = lax.axis_index(("z", "y", "core"))
    zy = lax.axis_size("z") * lax.axis_size("y")
    shape = jax.ShapeDtypeStruct
    places = jnp.stack([core, x0, x1, slab])

    other_core, other_x0 = [(0, 1), (1, 0)], [(0, 1), (1, 0)]

    partner = lax.ppermute(integrals, ("x1", "x0"), [(0, 3), (3, 0), (1, 2), (2, 1)])

    steps = 4
    cut = pl.pallas_call(
        functools.partial(cut_body, steps),
        in_specs=[pl.BlockSpec(memory_space=pl.ANY)] * 2,
        out_specs=pl.BlockSpec(memory_space=pl.ANY),
        out_shape=shape((2 * zy, 8, LANES), BF16),
        scratch_shapes=[
            pltpu.SMEM(pair_irrep.shape, jnp.int32),
            pltpu.VMEM(amplitudes.shape, BF16),
            pltpu.VMEM((2 * zy, 8, LANES), BF16),
            pltpu.SemaphoreType.DMA,
            pltpu.SemaphoreType.DMA((steps,)),
            pltpu.SemaphoreType.DMA((steps,)),
        ],
        cost_estimate=pl.CostEstimate(flops=0, bytes_accessed=700000, transcendentals=0),
    )(pair_irrep, amplitudes)
    cut, block = lax.optimization_barrier((cut, integrals))
    mine = lax.all_to_all(cut.reshape(zy, 16, LANES), ("z", "y"), 0, 0, tiled=True)
    mine = mine.reshape(zy, 2, 8, LANES)
    there = lax.ppermute(mine, "x0", other_x0)

    rows_f32, rows_bf16 = pltpu.VMEM((zy, WIDE), F32), shape((2 * zy, NV), BF16)
    flat, all_f32 = pltpu.VMEM((zy * 8, LANES), F32), shape((2 * zy, NV), F32)

    def rows(tiles, nbytes):
        out = [shape((zy, NV), BF16), shape((zy, NV), F32)]
        body = functools.partial(rows_body, zy)
        return call(body, out, "ssvvv", nbytes * 300, nbytes, [flat, rows_f32])(
            places, slab_irrep, virt_irrep, tiles, integrals
        )

    lhs_here, sums_here = rows(mine, 3000000)
    block2 = lax.ppermute(block, "core", other_core)
    partner, sums_here = lax.optimization_barrier((partner, sums_here))
    partner2 = lax.ppermute(partner, "core", other_core)
    lhs_there, sums_there = rows(there, 20000000)
    other = call(
        functools.partial(other_body, zy),
        [rows_bf16, shape((2 * zy * 8, LANES), F32)],
        "ssvvvvvv",
        1000,
        3000000,
        [flat, rows_f32, pltpu.VMEM((2 * zy, NV), F32)],
    )
    lhs2, own_sums = other(places, slab_irrep, virt_irrep, mine, there, block2, sums_here, sums_there)
    first = call(
        functools.partial(partner_body, zy), all_f32, "svvv", 6000000000, 20000000, [pltpu.VMEM((2 * zy, NV), BF16)]
    )
    ladder = call(
        functools.partial(ladder_body, zy), shape((2 * zy * 16, LANES), F32), "vvvv", 1000, 3000000
    )
    part = ladder(lhs2, partner2, first(places, lhs_here, lhs_there, partner), own_sums)
    part = (part * SCALE).astype(F16).reshape(2 * zy, 16, LANES)
    back = lax.all_to_all(part, ("x0", "z", "y"), 0, 0, tiled=True)
    sums = jnp.sum(back.reshape(2, zy, 16, LANES).astype(F32), axis=1)
    finish = call(finish_body, shape((1, 4 * NV), BF16), "sssvvv", 0, 50000)
    return finish(places, pair_irrep, upper_irrep, sums, virt_irrep, residual_in)


def solution(mesh):
    fine = Mesh(mesh.devices.reshape(8, 8, 2, 2, 2), AXES)
    return jax.shard_map(
        per_device,
        mesh=fine,
        in_specs=(P(AXES, None), P(AXES[:3], AXES[3:]), P(AXES, None), P(AXES), P(), P(), P()),
        out_specs=P(AXES, None),
        check_vma=False,
    )
```

```python
import functools

import jax
import jax.numpy as jnp
from jax import lax
from jax.experimental import pallas as pl
from jax.experimental.pallas import tpu as pltpu
from jax.sharding import Mesh
from jax.sharding import PartitionSpec as P

AXES = ("z", "y", "core", "x1", "x0")
BF16, F32, F16 = jnp.bfloat16, jnp.float32, jnp.float16
NV = 800
LANES = 128
TILES = 7
WIDE = TILES * LANES
SCALE = 64.0

VMEM = pl.BlockSpec(memory_space=pltpu.VMEM)
SMEM = pl.BlockSpec(memory_space=pltpu.SMEM)


def call(body, out, ins, flops, nbytes, scratch=()):
    return pl.pallas_call(
        body,
        out_shape=out,
        in_specs=[SMEM if kind == "s" else VMEM for kind in ins],
        out_specs=jax.tree.map(lambda _: VMEM, out),
        scratch_shapes=list(scratch),
        compiler_params=pltpu.CompilerParams(vmem_limit_bytes=16 * 1024 * 1024),
        cost_estimate=pl.CostEstimate(flops=flops, bytes_accessed=nbytes, transcendentals=0),
    )


def cut_body(steps, pair_ref, row_ref, out_ref, pair, row, cut, pair_sem, in_sems, out_sems):
    lanes, slabs = row.shape[1] // steps, cut.shape[0] // steps

    def fetch(i):
        part = pl.ds(i * lanes, lanes)
        return pltpu.make_async_copy(row_ref.at[:, part], row.at[:, part], in_sems.at[i])

    def put(i):
        part = pl.ds(i * slabs, slabs)
        return pltpu.make_async_copy(cut.at[part], out_ref.at[part], out_sems.at[i])

    label = pltpu.make_async_copy(pair_ref, pair, pair_sem)
    label.start()

    def four(q, carry):
        for r in range(4):
            at = [pl.multiple_of(q * 3200 + (6 * r + t) * LANES, LANES) for t in range(TILES)]
            tiles = [row[:, pl.ds(a, LANES)].astype(F32) for a in at]
            cut[4 * q + r] = jnp.concatenate(tiles + [filler], axis=0).astype(BF16)
        return carry

    for i in range(steps):
        fetch(i).start()
    label.wait()
    filler = jnp.full((1, LANES), pair[0].astype(F32))
    for i in range(steps):
        fetch(i).wait()
        lax.fori_loop(i * slabs // 4, (i + 1) * slabs // 4, four, 0, unroll=4)
        put(i).start()
    for i in range(steps):
        put(i).wait()


def put_tiles(sums, count, out_ref, first, step):
    wide = jnp.concatenate([sums, jnp.zeros((count, WIDE - NV), F32)], axis=1)
    for t in range(TILES):
        out_ref[pl.ds(first + t, count, stride=step), :] = wide[:, t * LANES : (t + 1) * LANES]
    out_ref[pl.ds(first + TILES, count, stride=step), :] = jnp.zeros((count, LANES), F32)


def kept_rows(flip, zy, places_ref, slab_ref, virt_ref, tiles_ref, flat, wide, lhs_ref, first):
    c = jnp.bitwise_xor(places_ref[3], flip)
    flat[...] = tiles_ref[:, jnp.bitwise_xor(places_ref[0], flip)].astype(F32).reshape(zy * 8, LANES)
    for t in range(TILES):
        wide[:, t * LANES : (t + 1) * LANES] = flat[pl.ds(t, zy, stride=8), :]
    pair = flat[pl.ds(TILES, zy, stride=8), :][:, 0:1]
    cd = jnp.bitwise_xor(virt_ref[...].reshape(1, NV), slab_ref[c]).astype(F32)
    for shift in range(4):

        @pl.when(c % 4 == shift)
        def _():
            row = wide[:, 32 * shift : 32 * shift + NV]
            lhs_ref[pl.ds(first, zy), :] = jnp.where(pair == cd, row, 0.0).astype(BF16)


def rows_body(zy, places_ref, slab_ref, virt_ref, tiles_ref, own_ref, lhs_ref, lhs2_ref, out_ref, flat, wide):
    kept_rows(0, zy, places_ref, slab_ref, virt_ref, tiles_ref, flat, wide, lhs_ref, 0)
    out_ref[...] = jnp.dot(lhs_ref[...], own_ref[...], preferred_element_type=F32)
    kept_rows(1, zy, places_ref, slab_ref, virt_ref, tiles_ref, flat, wide, lhs2_ref, 0)


def there_body(zy, *refs):
    places_ref, slab_ref, virt_ref, tiles_ref, lhs_ref, lhs2_ref, sums_ref = refs[:7]
    own_ref, own2_ref, block_ref = refs[7:10]
    rows2_ref, own_sums_ref, out_ref, flat, wide, rows, sums = refs[10:]
    here = pl.multiple_of(places_ref[1] * zy, zy)
    there = pl.multiple_of(zy - here, zy)
    rows[pl.ds(here, zy), :] = lhs_ref[...]
    rows2_ref[pl.ds(here, zy), :] = lhs2_ref[...]
    sums[pl.ds(here, zy), :] = sums_ref[...]
    kept_rows(0, zy, places_ref, slab_ref, virt_ref, tiles_ref, flat, wide, rows, there)
    kept_rows(1, zy, places_ref, slab_ref, virt_ref, tiles_ref, flat, wide, rows2_ref, there)
    own = jnp.dot(rows[pl.ds(there, zy), :], own_ref[...], preferred_element_type=F32)
    sums[pl.ds(there, zy), :] = own
    own = sums[...] + jnp.dot(rows2_ref[...], own2_ref[...], preferred_element_type=F32)
    put_tiles(own, 2 * zy, own_sums_ref, 0, 8)
    out_ref[...] = jnp.dot(rows[...], block_ref[...], preferred_element_type=F32)


def ladder_body(zy, lhs_ref, block_ref, sums_ref, own_ref, out_ref):
    sums = sums_ref[...] + jnp.dot(lhs_ref[...], block_ref[...], preferred_element_type=F32)
    put_tiles(sums, 2 * zy, out_ref, 8, 16)
    for t in range(8):
        out_ref[pl.ds(t, 2 * zy, stride=16), :] = own_ref[pl.ds(t, 2 * zy, stride=8), :]


def finish_body(places_ref, sums_ref, kept_ref, old_ref, out_ref):
    swap = places_ref[2] == 1
    order = ((0, 0), (1, 0), (1, 1), (0, 1))
    for a in range(4):
        s, h = order[a]
        s2, h2 = order[(a + 2) % 4]
        straight = sums_ref[s, 8 * h : 8 * h + 8, :]
        turned = sums_ref[s2, 8 * h2 : 8 * h2 + 8, :]
        tiles = jnp.where(swap, turned, straight) * (1.0 / SCALE)
        row = jnp.concatenate([tiles[t : t + 1, :] for t in range(TILES)], axis=1)[:, :NV]
        row = jnp.where(kept_ref[a : a + 1, :] > 0.5, row, 0.0)
        old = old_ref[:, a * NV : (a + 1) * NV].astype(F32)
        out_ref[:, a * NV : (a + 1) * NV] = (old + row).astype(BF16)


def per_device(amplitudes, integrals, residual_in, pair_irrep, slab_irrep, upper_irrep, virt_irrep):
    core = lax.axis_index("core")
    x1 = lax.axis_index("x1")
    x0 = lax.axis_index("x0")
    slab = lax.axis_index(("z", "y", "core"))
    zy = lax.axis_size("z") * lax.axis_size("y")
    shape = jax.ShapeDtypeStruct
    places = jnp.stack([core, x0, x1, slab])

    other_core, other_x0 = [(0, 1), (1, 0)], [(0, 1), (1, 0)]

    partner = lax.ppermute(integrals, ("x1", "x0"), [(0, 3), (3, 0), (1, 2), (2, 1)])

    steps = 4
    cut = pl.pallas_call(
        functools.partial(cut_body, steps),
        in_specs=[pl.BlockSpec(memory_space=pltpu.HBM)] * 2,
        out_specs=pl.BlockSpec(memory_space=pltpu.HBM),
        out_shape=shape((2 * zy, 8, LANES), BF16),
        scratch_shapes=[
            pltpu.SMEM(pair_irrep.shape, jnp.int32),
            pltpu.VMEM(amplitudes.shape, BF16),
            pltpu.VMEM((2 * zy, 8, LANES), BF16),
            pltpu.SemaphoreType.DMA,
            pltpu.SemaphoreType.DMA((steps,)),
            pltpu.SemaphoreType.DMA((steps,)),
        ],
        cost_estimate=pl.CostEstimate(flops=0, bytes_accessed=700000, transcendentals=0),
    )(pair_irrep, amplitudes)
    cut, block = lax.optimization_barrier((cut, integrals))
    mine = lax.all_to_all(cut.reshape(zy, 16, LANES), ("z", "y"), 0, 0, tiled=True)
    mine = mine.reshape(zy, 2, 8, LANES)
    there = lax.ppermute(mine, "x0", other_x0)

    flat, wide = pltpu.VMEM((zy * 8, LANES), F32), pltpu.VMEM((zy, WIDE), F32)
    half, whole = shape((zy, NV), BF16), shape((2 * zy, NV), BF16)
    rows = call(
        functools.partial(rows_body, zy),
        [half, half, shape((zy, NV), F32)],
        "ssvvv",
        24000000 * 300,
        24000000,
        [flat, wide],
    )
    lhs, lhs2, sums = rows(places, slab_irrep, virt_irrep, mine, integrals)
    block2 = lax.ppermute(block, "core", other_core)
    partner, sums = lax.optimization_barrier((partner, sums))
    partner2 = lax.ppermute(partner, "core", other_core)
    after = call(
        functools.partial(there_body, zy),
        [whole, shape((2 * zy * 8, LANES), F32), shape((2 * zy, NV), F32)],
        "ssvvvvvvvv",
        40000000 * 300,
        40000000,
        [flat, wide, pltpu.VMEM((2 * zy, NV), BF16), pltpu.VMEM((2 * zy, NV), F32)],
    )
    rows2, own_sums, sums = after(
        places, slab_irrep, virt_irrep, there, lhs, lhs2, sums, integrals, block2, partner
    )
    ladder = call(
        functools.partial(ladder_body, zy), shape((2 * zy * 16, LANES), F32), "vvvv", 1000, 3000000
    )
    part = ladder(rows2, partner2, sums, own_sums)
    part = (part * SCALE).astype(F16).reshape(2 * zy, 16, LANES)
    part, upper = lax.optimization_barrier((part, upper_irrep))
    back = lax.all_to_all(part, ("x0", "z", "y"), 0, 0, tiled=True)
    ab_irrep = jnp.bitwise_xor(upper[:, None], virt_irrep[None, :])
    kept = (ab_irrep == cut[0, TILES, 0].astype(jnp.int32)).astype(F32)
    sums = jnp.sum(back.reshape(2, zy, 16, LANES).astype(F32), axis=1)
    finish = call(finish_body, shape((1, 4 * NV), BF16), "svvv", 0, 50000)
    return finish(places, sums, kept, residual_in)


def solution(mesh):
    fine = Mesh(mesh.devices.reshape(8, 8, 2, 2, 2), AXES)
    return jax.shard_map(
        per_device,
        mesh=fine,
        in_specs=(P(AXES, None), P(AXES[:3], AXES[3:]), P(AXES, None), P(AXES), P(), P(), P()),
        out_specs=P(AXES, None),
        check_vma=False,
    )
```

```python
import functools

import jax
import jax.numpy as jnp
from jax import lax
from jax.experimental import pallas as pl
from jax.experimental.pallas import tpu as pltpu
from jax.sharding import Mesh
from jax.sharding import PartitionSpec as P

AXES = ("z", "y", "core", "x1", "x0")
BF16, F32, F16 = jnp.bfloat16, jnp.float32, jnp.float16
NV = 800
LANES = 128
TILES = 7
WIDE = TILES * LANES
SCALE = 64.0

VMEM = pl.BlockSpec(memory_space=pltpu.VMEM)
SMEM = pl.BlockSpec(memory_space=pltpu.SMEM)


def call(body, out, ins, flops, nbytes, scratch=()):
    return pl.pallas_call(
        body,
        out_shape=out,
        in_specs=[SMEM if kind == "s" else VMEM for kind in ins],
        out_specs=jax.tree.map(lambda _: VMEM, out),
        scratch_shapes=list(scratch),
        compiler_params=pltpu.CompilerParams(vmem_limit_bytes=16 * 1024 * 1024),
        cost_estimate=pl.CostEstimate(flops=flops, bytes_accessed=nbytes, transcendentals=0),
    )


def cut_body(steps, pair_ref, row_ref, out_ref, pair, row, cut, pair_sem, in_sems, out_sems):
    lanes, slabs = row.shape[1] // steps, cut.shape[0] // steps

    def fetch(i):
        part = pl.ds(i * lanes, lanes)
        return pltpu.make_async_copy(row_ref.at[:, part], row.at[:, part], in_sems.at[i])

    def put(i):
        part = pl.ds(i * slabs, slabs)
        return pltpu.make_async_copy(cut.at[part], out_ref.at[part], out_sems.at[i])

    label = pltpu.make_async_copy(pair_ref, pair, pair_sem)
    label.start()

    def four(q, carry):
        for r in range(4):
            at = [pl.multiple_of(q * 3200 + (6 * r + t) * LANES, LANES) for t in range(TILES)]
            tiles = [row[:, pl.ds(a, LANES)].astype(F32) for a in at]
            cut[4 * q + r] = jnp.concatenate(tiles + [filler], axis=0).astype(BF16)
        return carry

    for i in range(steps):
        fetch(i).start()
    label.wait()
    filler = jnp.full((1, LANES), pair[0].astype(F32))
    for i in range(steps):
        fetch(i).wait()
        lax.fori_loop(i * slabs // 4, (i + 1) * slabs // 4, four, 0, unroll=4)
        put(i).start()
    for i in range(steps):
        put(i).wait()


def put_tiles(sums, count, out_ref, first, step):
    wide = jnp.concatenate([sums, jnp.zeros((count, WIDE - NV), F32)], axis=1)
    for t in range(TILES):
        out_ref[pl.ds(first + t, count, stride=step), :] = wide[:, t * LANES : (t + 1) * LANES]
    out_ref[pl.ds(first + TILES, count, stride=step), :] = jnp.zeros((count, LANES), F32)


def kept_rows(flip, zy, places_ref, slab_ref, virt_ref, tiles_ref, flat, wide, lhs_ref, first):
    c = jnp.bitwise_xor(places_ref[3], flip)
    flat[...] = tiles_ref[:, jnp.bitwise_xor(places_ref[0], flip)].astype(F32).reshape(zy * 8, LANES)
    for t in range(TILES):
        wide[:, t * LANES : (t + 1) * LANES] = flat[pl.ds(t, zy, stride=8), :]
    pair = flat[pl.ds(TILES, zy, stride=8), :][:, 0:1]
    cd = jnp.bitwise_xor(virt_ref[...].reshape(1, NV), slab_ref[c]).astype(F32)
    for shift in range(4):

        @pl.when(c % 4 == shift)
        def _():
            row = wide[:, 32 * shift : 32 * shift + NV]
            lhs_ref[pl.ds(first, zy), :] = jnp.where(pair == cd, row, 0.0).astype(BF16)


def rows_body(zy, places_ref, slab_ref, virt_ref, tiles_ref, own_ref, lhs_ref, lhs2_ref, out_ref, flat, wide):
    kept_rows(0, zy, places_ref, slab_ref, virt_ref, tiles_ref, flat, wide, lhs_ref, 0)
    out_ref[...] = jnp.dot(lhs_ref[...], own_ref[...], preferred_element_type=F32)
    kept_rows(1, zy, places_ref, slab_ref, virt_ref, tiles_ref, flat, wide, lhs2_ref, 0)


def there_body(zy, *refs):
    places_ref, slab_ref, virt_ref, tiles_ref, lhs_ref, lhs2_ref, sums_ref = refs[:7]
    own_ref, own2_ref, block_ref = refs[7:10]
    rows2_ref, own_sums_ref, out_ref, flat, wide, rows, sums = refs[10:]
    here = pl.multiple_of(places_ref[1] * zy, zy)
    there = pl.multiple_of(zy - here, zy)
    rows[pl.ds(here, zy), :] = lhs_ref[...]
    rows2_ref[pl.ds(here, zy), :] = lhs2_ref[...]
    sums[pl.ds(here, zy), :] = sums_ref[...]
    kept_rows(0, zy, places_ref, slab_ref, virt_ref, tiles_ref, flat, wide, rows, there)
    kept_rows(1, zy, places_ref, slab_ref, virt_ref, tiles_ref, flat, wide, rows2_ref, there)
    own = jnp.dot(rows[pl.ds(there, zy), :], own_ref[...], preferred_element_type=F32)
    sums[pl.ds(there, zy), :] = own
    own = sums[...] + jnp.dot(rows2_ref[...], own2_ref[...], preferred_element_type=F32)
    put_tiles(own, 2 * zy, own_sums_ref, 0, 8)
    out_ref[...] = jnp.dot(rows[...], block_ref[...], preferred_element_type=F32)


def ladder_body(zy, lhs_ref, block_ref, sums_ref, own_ref, out_ref):
    sums = sums_ref[...] + jnp.dot(lhs_ref[...], block_ref[...], preferred_element_type=F32)
    put_tiles(sums, 2 * zy, out_ref, 8, 16)
    for t in range(8):
        out_ref[pl.ds(t, 2 * zy, stride=16), :] = own_ref[pl.ds(t, 2 * zy, stride=8), :]


def finish_body(places_ref, sums_ref, kept_ref, old_ref, out_ref):
    swap = places_ref[2] == 1
    order = ((0, 0), (1, 0), (1, 1), (0, 1))
    for a in range(4):
        s, h = order[a]
        s2, h2 = order[(a + 2) % 4]
        straight = sums_ref[s, 8 * h : 8 * h + 8, :]
        turned = sums_ref[s2, 8 * h2 : 8 * h2 + 8, :]
        tiles = jnp.where(swap, turned, straight) * (1.0 / SCALE)
        row = jnp.concatenate([tiles[t : t + 1, :] for t in range(TILES)], axis=1)[:, :NV]
        row = jnp.where(kept_ref[a : a + 1, :] > 0.5, row, 0.0)
        old = old_ref[:, a * NV : (a + 1) * NV].astype(F32)
        out_ref[:, a * NV : (a + 1) * NV] = (old + row).astype(BF16)


def per_device(amplitudes, integrals, residual_in, pair_irrep, slab_irrep, upper_irrep, virt_irrep):
    core = lax.axis_index("core")
    x1 = lax.axis_index("x1")
    x0 = lax.axis_index("x0")
    slab = lax.axis_index(("z", "y", "core"))
    zy = lax.axis_size("z") * lax.axis_size("y")
    shape = jax.ShapeDtypeStruct
    places = jnp.stack([core, x0, x1, slab])

    other_core, other_x0 = [(0, 1), (1, 0)], [(0, 1), (1, 0)]

    partner = lax.ppermute(integrals, ("x1", "x0"), [(0, 3), (3, 0), (1, 2), (2, 1)])

    steps = 4
    cut = pl.pallas_call(
        functools.partial(cut_body, steps),
        in_specs=[pl.BlockSpec(memory_space=pltpu.HBM)] * 2,
        out_specs=pl.BlockSpec(memory_space=pltpu.HBM),
        out_shape=shape((2 * zy, 8, LANES), BF16),
        scratch_shapes=[
            pltpu.SMEM(pair_irrep.shape, jnp.int32),
            pltpu.VMEM(amplitudes.shape, BF16),
            pltpu.VMEM((2 * zy, 8, LANES), BF16),
            pltpu.SemaphoreType.DMA,
            pltpu.SemaphoreType.DMA((steps,)),
            pltpu.SemaphoreType.DMA((steps,)),
        ],
        cost_estimate=pl.CostEstimate(flops=0, bytes_accessed=700000, transcendentals=0),
    )(pair_irrep, amplitudes)
    cut, block = lax.optimization_barrier((cut, integrals))
    mine = lax.all_to_all(cut.reshape(zy, 16, LANES), ("z", "y"), 0, 0, tiled=True)
    mine = mine.reshape(zy, 2, 8, LANES)
    there = lax.ppermute(mine, "x0", other_x0)

    flat, wide = pltpu.VMEM((zy * 8, LANES), F32), pltpu.VMEM((zy, WIDE), F32)
    half, whole = shape((zy, NV), BF16), shape((2 * zy, NV), BF16)
    rows = call(
        functools.partial(rows_body, zy),
        [half, half, shape((zy, NV), F32)],
        "ssvvv",
        24000000 * 300,
        24000000,
        [flat, wide],
    )
    lhs, lhs2, sums = rows(places, slab_irrep, virt_irrep, mine, integrals)
    block2 = lax.ppermute(block, "core", other_core)
    partner, sums = lax.optimization_barrier((partner, sums))
    partner2 = lax.ppermute(partner, "core", other_core)
    after = call(
        functools.partial(there_body, zy),
        [whole, shape((2 * zy * 8, LANES), F32), shape((2 * zy, NV), F32)],
        "ssvvvvvvvv",
        40000000 * 300,
        40000000,
        [flat, wide, pltpu.VMEM((2 * zy, NV), BF16), pltpu.VMEM((2 * zy, NV), F32)],
    )
    rows2, own_sums, sums = after(
        places, slab_irrep, virt_irrep, there, lhs, lhs2, sums, integrals, block2, partner
    )
    ladder = call(
        functools.partial(ladder_body, zy), shape((2 * zy * 16, LANES), F32), "vvvv", 1000, 3000000
    )
    part = ladder(rows2, partner2, sums, own_sums)
    num_z, num_y = lax.axis_size("z"), lax.axis_size("y")
    part = (part * SCALE).astype(F16).reshape(2, num_z, num_y, 16, LANES)
    part = jnp.transpose(part, (2, 0, 1, 3, 4)).reshape(num_y, 2 * num_z * 16, LANES)
    back = lax.all_to_all(part, "y", 0, 0, tiled=True)
    sums = jnp.sum(back.astype(F32), axis=0).reshape(2 * num_z, 16, LANES)
    sums = lax.all_to_all(sums, ("x0", "z"), 0, 0, tiled=True)
    sums = jnp.sum(sums.reshape(2, num_z, 16, LANES), axis=1)
    ab_irrep = jnp.bitwise_xor(upper_irrep[:, None], virt_irrep[None, :])
    kept = (ab_irrep == cut[0, TILES, 0].astype(jnp.int32)).astype(F32)
    finish = call(finish_body, shape((1, 4 * NV), BF16), "svvv", 0, 50000)
    return finish(places, sums, kept, residual_in)


def solution(mesh):
    fine = Mesh(mesh.devices.reshape(8, 8, 2, 2, 2), AXES)
    return jax.shard_map(
        per_device,
        mesh=fine,
        in_specs=(P(AXES, None), P(AXES[:3], AXES[3:]), P(AXES, None), P(AXES), P(), P(), P()),
        out_specs=P(AXES, None),
        check_vma=False,
    )
```

```python
import functools

import jax
import jax.numpy as jnp
from jax import lax
from jax.experimental import pallas as pl
from jax.experimental.pallas import tpu as pltpu
from jax.sharding import Mesh
from jax.sharding import PartitionSpec as P

AXES = ("z", "y", "core", "x1", "x0")
BF16, F32, F16 = jnp.bfloat16, jnp.float32, jnp.float16
NV = 800
LANES = 128
TILES = 7
WIDE = TILES * LANES
ROLLED = [(z + 4) % 8 * 8 + (y + 4) % 8 for z in range(8) for y in range(8)]
SCALE = 64.0

VMEM = pl.BlockSpec(memory_space=pltpu.VMEM)
SMEM = pl.BlockSpec(memory_space=pltpu.SMEM)


def call(body, out, ins, flops, nbytes, scratch=()):
    return pl.pallas_call(
        body,
        out_shape=out,
        in_specs=[SMEM if kind == "s" else VMEM for kind in ins],
        out_specs=jax.tree.map(lambda _: VMEM, out),
        scratch_shapes=list(scratch),
        compiler_params=pltpu.CompilerParams(vmem_limit_bytes=16 * 1024 * 1024),
        cost_estimate=pl.CostEstimate(flops=flops, bytes_accessed=nbytes, transcendentals=0),
    )


def cut_body(steps, pair_ref, row_ref, out_ref, pair, row, cut, pair_sem, in_sems, out_sems):
    lanes, slabs = row.shape[1] // steps, cut.shape[0] // steps

    def fetch(i):
        part = pl.ds(i * lanes, lanes)
        return pltpu.make_async_copy(row_ref.at[:, part], row.at[:, part], in_sems.at[i])

    def put(i):
        part = pl.ds(i * slabs, slabs)
        return pltpu.make_async_copy(cut.at[part], out_ref.at[part], out_sems.at[i])

    label = pltpu.make_async_copy(pair_ref, pair, pair_sem)
    label.start()

    def four(q, carry):
        for r in range(4):
            at = [pl.multiple_of(q * 3200 + (6 * r + t) * LANES, LANES) for t in range(TILES)]
            tiles = [row[:, pl.ds(a, LANES)].astype(F32) for a in at]
            chip = 2 * q + r // 2
            place = (chip // 8 + 4) % 8 * 8 + (chip + 4) % 8
            cut[2 * place + r % 2] = jnp.concatenate(tiles + [filler], axis=0).astype(BF16)
        return carry

    for i in range(steps):
        fetch(i).start()
    label.wait()
    filler = jnp.full((1, LANES), pair[0].astype(F32))
    for i in range(steps):
        fetch(i).wait()
        lax.fori_loop(i * slabs // 4, (i + 1) * slabs // 4, four, 0, unroll=4)
        put((i + 2) % 4).start()
    for i in range(steps):
        put(i).wait()


def put_tiles(sums, count, out_ref, first, step):
    wide = jnp.concatenate([sums, jnp.zeros((count, WIDE - NV), F32)], axis=1)
    for t in range(TILES):
        out_ref[pl.ds(first + t, count, stride=step), :] = wide[:, t * LANES : (t + 1) * LANES]
    out_ref[pl.ds(first + TILES, count, stride=step), :] = jnp.zeros((count, LANES), F32)


def kept_rows(flip, zy, places_ref, slab_ref, virt_ref, tiles_ref, flat, wide, lhs_ref, first):
    c = jnp.bitwise_xor(places_ref[3], flip)
    flat[...] = tiles_ref[:, jnp.bitwise_xor(places_ref[0], flip)].astype(F32).reshape(zy * 8, LANES)
    for t in range(TILES):
        wide[:, t * LANES : (t + 1) * LANES] = flat[pl.ds(t, zy, stride=8), :]
    pair = flat[pl.ds(TILES, zy, stride=8), :][:, 0:1]
    cd = jnp.bitwise_xor(virt_ref[...].reshape(1, NV), slab_ref[c]).astype(F32)
    for shift in range(4):

        @pl.when(c % 4 == shift)
        def _():
            row = wide[:, 32 * shift : 32 * shift + NV]
            lhs_ref[pl.ds(first, zy), :] = jnp.where(pair == cd, row, 0.0).astype(BF16)


def rows_body(zy, places_ref, slab_ref, virt_ref, tiles_ref, own_ref, lhs_ref, lhs2_ref, out_ref, flat, wide):
    kept_rows(0, zy, places_ref, slab_ref, virt_ref, tiles_ref, flat, wide, lhs_ref, 0)
    out_ref[...] = jnp.dot(lhs_ref[...], own_ref[...], preferred_element_type=F32)
    kept_rows(1, zy, places_ref, slab_ref, virt_ref, tiles_ref, flat, wide, lhs2_ref, 0)


def there_body(zy, *refs):
    places_ref, slab_ref, virt_ref, tiles_ref, lhs_ref, lhs2_ref, sums_ref = refs[:7]
    own_ref, own2_ref, block_ref = refs[7:10]
    rows2_ref, own_sums_ref, out_ref, flat, wide, rows, sums = refs[10:]
    here = pl.multiple_of(places_ref[1] * zy, zy)
    there = pl.multiple_of(zy - here, zy)
    rows[pl.ds(here, zy), :] = lhs_ref[...]
    rows2_ref[pl.ds(here, zy), :] = lhs2_ref[...]
    sums[pl.ds(here, zy), :] = sums_ref[...]
    kept_rows(0, zy, places_ref, slab_ref, virt_ref, tiles_ref, flat, wide, rows, there)
    kept_rows(1, zy, places_ref, slab_ref, virt_ref, tiles_ref, flat, wide, rows2_ref, there)
    own = jnp.dot(rows[pl.ds(there, zy), :], own_ref[...], preferred_element_type=F32)
    sums[pl.ds(there, zy), :] = own
    own = sums[...] + jnp.dot(rows2_ref[...], own2_ref[...], preferred_element_type=F32)
    put_tiles(own, 2 * zy, own_sums_ref, 0, 8)
    out_ref[...] = jnp.dot(rows[...], block_ref[...], preferred_element_type=F32)


def ladder_body(zy, lhs_ref, block_ref, sums_ref, own_ref, out_ref):
    sums = sums_ref[...] + jnp.dot(lhs_ref[...], block_ref[...], preferred_element_type=F32)
    put_tiles(sums, 2 * zy, out_ref, 8, 16)
    for t in range(8):
        out_ref[pl.ds(t, 2 * zy, stride=16), :] = own_ref[pl.ds(t, 2 * zy, stride=8), :]


def finish_body(places_ref, sums_ref, kept_ref, old_ref, out_ref):
    swap = places_ref[2] == 1
    order = ((0, 0), (1, 0), (1, 1), (0, 1))
    for a in range(4):
        s, h = order[a]
        s2, h2 = order[(a + 2) % 4]
        straight = sums_ref[s, 8 * h : 8 * h + 8, :]
        turned = sums_ref[s2, 8 * h2 : 8 * h2 + 8, :]
        tiles = jnp.where(swap, turned, straight) * (1.0 / SCALE)
        row = jnp.concatenate([tiles[t : t + 1, :] for t in range(TILES)], axis=1)[:, :NV]
        row = jnp.where(kept_ref[a : a + 1, :] > 0.5, row, 0.0)
        old = old_ref[:, a * NV : (a + 1) * NV].astype(F32)
        out_ref[:, a * NV : (a + 1) * NV] = (old + row).astype(BF16)


def per_device(amplitudes, integrals, residual_in, pair_irrep, slab_irrep, upper_irrep, virt_irrep):
    core = lax.axis_index("core")
    x1 = lax.axis_index("x1")
    x0 = lax.axis_index("x0")
    slab = lax.axis_index(("z", "y", "core"))
    zy = lax.axis_size("z") * lax.axis_size("y")
    shape = jax.ShapeDtypeStruct
    places = jnp.stack([core, x0, x1, slab])

    other_core, other_x0 = [(0, 1), (1, 0)], [(0, 1), (1, 0)]

    partner = lax.ppermute(integrals, ("x1", "x0"), [(0, 3), (3, 0), (1, 2), (2, 1)])

    steps = 4
    cut = pl.pallas_call(
        functools.partial(cut_body, steps),
        in_specs=[pl.BlockSpec(memory_space=pltpu.HBM)] * 2,
        out_specs=pl.BlockSpec(memory_space=pltpu.HBM),
        out_shape=shape((2 * zy, 8, LANES), BF16),
        scratch_shapes=[
            pltpu.SMEM(pair_irrep.shape, jnp.int32),
            pltpu.VMEM(amplitudes.shape, BF16),
            pltpu.VMEM((2 * zy, 8, LANES), BF16),
            pltpu.SemaphoreType.DMA,
            pltpu.SemaphoreType.DMA((steps,)),
            pltpu.SemaphoreType.DMA((steps,)),
        ],
        cost_estimate=pl.CostEstimate(flops=0, bytes_accessed=700000, transcendentals=0),
    )(pair_irrep, amplitudes)
    cut, block = lax.optimization_barrier((cut, integrals))
    mine = lax.all_to_all(
        cut.reshape(zy, 16, LANES), ("z", "y"), 0, 0, axis_index_groups=[ROLLED], tiled=True
    )
    mine = mine.reshape(zy, 2, 8, LANES)
    there = lax.ppermute(mine, "x0", other_x0)

    flat, wide = pltpu.VMEM((zy * 8, LANES), F32), pltpu.VMEM((zy, WIDE), F32)
    half, whole = shape((zy, NV), BF16), shape((2 * zy, NV), BF16)
    rows = call(
        functools.partial(rows_body, zy),
        [half, half, shape((zy, NV), F32)],
        "ssvvv",
        24000000 * 300,
        24000000,
        [flat, wide],
    )
    lhs, lhs2, sums = rows(places, slab_irrep, virt_irrep, mine, integrals)
    block2 = lax.ppermute(block, "core", other_core)
    partner, sums = lax.optimization_barrier((partner, sums))
    partner2 = lax.ppermute(partner, "core", other_core)
    after = call(
        functools.partial(there_body, zy),
        [whole, shape((2 * zy * 8, LANES), F32), shape((2 * zy, NV), F32)],
        "ssvvvvvvvv",
        40000000 * 300,
        40000000,
        [flat, wide, pltpu.VMEM((2 * zy, NV), BF16), pltpu.VMEM((2 * zy, NV), F32)],
    )
    rows2, own_sums, sums = after(
        places, slab_irrep, virt_irrep, there, lhs, lhs2, sums, integrals, block2, partner
    )
    ladder = call(
        functools.partial(ladder_body, zy), shape((2 * zy * 16, LANES), F32), "vvvv", 1000, 3000000
    )
    part = ladder(rows2, partner2, sums, own_sums)
    part = (part * SCALE).astype(F16).reshape(2 * zy, 16, LANES)
    part, upper = lax.optimization_barrier((part, upper_irrep))
    back = lax.all_to_all(
        part, ("x0", "z", "y"), 0, 0, axis_index_groups=[ROLLED + [64 + i for i in ROLLED]], tiled=True
    )
    ab_irrep = jnp.bitwise_xor(upper[:, None], virt_irrep[None, :])
    kept = (ab_irrep == cut[0, TILES, 0].astype(jnp.int32)).astype(F32)
    sums = jnp.sum(back.reshape(2, zy, 16, LANES).astype(F32), axis=1)
    finish = call(finish_body, shape((1, 4 * NV), BF16), "svvv", 0, 50000)
    return finish(places, sums, kept, residual_in)


def solution(mesh):
    fine = Mesh(mesh.devices.reshape(8, 8, 2, 2, 2), AXES)
    return jax.shard_map(
        per_device,
        mesh=fine,
        in_specs=(P(AXES, None), P(AXES[:3], AXES[3:]), P(AXES, None), P(AXES), P(), P(), P()),
        out_specs=P(AXES, None),
        check_vma=False,
    )
```

```python
import functools

import jax
import jax.numpy as jnp
from jax import lax
from jax.experimental import pallas as pl
from jax.experimental.pallas import tpu as pltpu
from jax.sharding import Mesh
from jax.sharding import PartitionSpec as P

AXES = ("z", "y", "core", "x1", "x0")
BF16, F32, F16 = jnp.bfloat16, jnp.float32, jnp.float16
NV = 800
LANES = 128
TILES = 7
WIDE = TILES * LANES
ROLLED = [(z + 4) % 8 * 8 + (y + 4) % 8 for z in range(8) for y in range(8)]
SCALE = 64.0

VMEM = pl.BlockSpec(memory_space=pltpu.VMEM)
SMEM = pl.BlockSpec(memory_space=pltpu.SMEM)


def call(body, out, ins, flops, nbytes, scratch=()):
    return pl.pallas_call(
        body,
        out_shape=out,
        in_specs=[SMEM if kind == "s" else VMEM for kind in ins],
        out_specs=jax.tree.map(lambda _: VMEM, out),
        scratch_shapes=list(scratch),
        compiler_params=pltpu.CompilerParams(vmem_limit_bytes=16 * 1024 * 1024),
        cost_estimate=pl.CostEstimate(flops=flops, bytes_accessed=nbytes, transcendentals=0),
    )


def cut_body(steps, pair_ref, row_ref, out_ref, pair, row, cut, pair_sem, in_sems, out_sems):
    lanes, slabs = row.shape[1] // steps, cut.shape[0] // steps

    def fetch(i):
        part = pl.ds(i * lanes, lanes)
        return pltpu.make_async_copy(row_ref.at[:, part], row.at[:, part], in_sems.at[i])

    def put(i):
        part = pl.ds(i * slabs, slabs)
        return pltpu.make_async_copy(cut.at[part], out_ref.at[part], out_sems.at[i])

    label = pltpu.make_async_copy(pair_ref, pair, pair_sem)
    label.start()

    def four(q, carry):
        for r in range(4):
            at = [pl.multiple_of(q * 3200 + (6 * r + t) * LANES, LANES) for t in range(TILES)]
            tiles = [row[:, pl.ds(a, LANES)].astype(F32) for a in at]
            chip = 2 * q + r // 2
            place = (chip // 8 + 4) % 8 * 8 + (chip + 4) % 8
            cut[2 * place + r % 2] = jnp.concatenate(tiles + [filler], axis=0).astype(BF16)
        return carry

    for i in range(steps):
        fetch(i).start()
    label.wait()
    filler = jnp.full((1, LANES), pair[0].astype(F32))
    for i in range(steps):
        fetch(i).wait()
        lax.fori_loop(i * slabs // 4, (i + 1) * slabs // 4, four, 0, unroll=4)
        put((i + 2) % 4).start()
    for i in range(steps):
        put(i).wait()


def put_tiles(sums, count, out_ref, first, step):
    wide = jnp.concatenate([sums, jnp.zeros((count, WIDE - NV), F32)], axis=1)
    for t in range(TILES):
        out_ref[pl.ds(first + t, count, stride=step), :] = wide[:, t * LANES : (t + 1) * LANES]
    out_ref[pl.ds(first + TILES, count, stride=step), :] = jnp.zeros((count, LANES), F32)


def kept_rows(flip, zy, places_ref, slab_ref, virt_ref, tiles_ref, flat, wide, lhs_ref, first):
    c = jnp.bitwise_xor(places_ref[3], flip)
    flat[...] = tiles_ref[:, jnp.bitwise_xor(places_ref[0], flip)].astype(F32).reshape(zy * 8, LANES)
    for t in range(TILES):
        wide[:, t * LANES : (t + 1) * LANES] = flat[pl.ds(t, zy, stride=8), :]
    pair = flat[pl.ds(TILES, zy, stride=8), :][:, 0:1]
    cd = jnp.bitwise_xor(virt_ref[...].reshape(1, NV), slab_ref[c]).astype(F32)
    for shift in range(4):

        @pl.when(c % 4 == shift)
        def _():
            row = wide[:, 32 * shift : 32 * shift + NV]
            lhs_ref[pl.ds(first, zy), :] = jnp.where(pair == cd, row, 0.0).astype(BF16)


def rows_body(zy, places_ref, slab_ref, virt_ref, tiles_ref, own_ref, lhs_ref, lhs2_ref, out_ref, flat, wide):
    kept_rows(0, zy, places_ref, slab_ref, virt_ref, tiles_ref, flat, wide, lhs_ref, 0)
    out_ref[...] = jnp.dot(lhs_ref[...], own_ref[...], preferred_element_type=F32)
    kept_rows(1, zy, places_ref, slab_ref, virt_ref, tiles_ref, flat, wide, lhs2_ref, 0)


def there_body(zy, *refs):
    places_ref, slab_ref, virt_ref, tiles_ref, lhs_ref, lhs2_ref, sums_ref = refs[:7]
    own_ref, own2_ref, block_ref = refs[7:10]
    rows2_ref, own_sums_ref, out_ref, flat, wide, rows, sums = refs[10:]
    here = pl.multiple_of(places_ref[1] * zy, zy)
    there = pl.multiple_of(zy - here, zy)
    rows[pl.ds(here, zy), :] = lhs_ref[...]
    rows2_ref[pl.ds(here, zy), :] = lhs2_ref[...]
    sums[pl.ds(here, zy), :] = sums_ref[...]
    kept_rows(0, zy, places_ref, slab_ref, virt_ref, tiles_ref, flat, wide, rows, there)
    kept_rows(1, zy, places_ref, slab_ref, virt_ref, tiles_ref, flat, wide, rows2_ref, there)
    own = jnp.dot(rows[pl.ds(there, zy), :], own_ref[...], preferred_element_type=F32)
    sums[pl.ds(there, zy), :] = own
    own = sums[...] + jnp.dot(rows2_ref[...], own2_ref[...], preferred_element_type=F32)
    put_tiles(own, 2 * zy, own_sums_ref, 0, 8)
    out_ref[...] = jnp.dot(rows[...], block_ref[...], preferred_element_type=F32)


def ladder_body(zy, lhs_ref, block_ref, sums_ref, own_ref, out_ref):
    sums = sums_ref[...] + jnp.dot(lhs_ref[...], block_ref[...], preferred_element_type=F32)
    put_tiles(sums, 2 * zy, out_ref, 8, 16)
    for t in range(8):
        out_ref[pl.ds(t, 2 * zy, stride=16), :] = own_ref[pl.ds(t, 2 * zy, stride=8), :]


def finish_body(places_ref, sums_ref, kept_ref, old_ref, out_ref):
    swap = places_ref[2] == 1
    order = ((0, 0), (1, 0), (1, 1), (0, 1))
    for a in range(4):
        s, h = order[a]
        s2, h2 = order[(a + 2) % 4]
        straight = sums_ref[s, 8 * h : 8 * h + 8, :]
        turned = sums_ref[s2, 8 * h2 : 8 * h2 + 8, :]
        tiles = jnp.where(swap, turned, straight) * (1.0 / SCALE)
        row = jnp.concatenate([tiles[t : t + 1, :] for t in range(TILES)], axis=1)[:, :NV]
        row = jnp.where(kept_ref[a : a + 1, :] > 0.5, row, 0.0)
        old = old_ref[:, a * NV : (a + 1) * NV].astype(F32)
        out_ref[:, a * NV : (a + 1) * NV] = (old + row).astype(BF16)


def per_device(amplitudes, integrals, residual_in, pair_irrep, slab_irrep, upper_irrep, virt_irrep):
    core = lax.axis_index("core")
    x1 = lax.axis_index("x1")
    x0 = lax.axis_index("x0")
    slab = lax.axis_index(("z", "y", "core"))
    zy = lax.axis_size("z") * lax.axis_size("y")
    shape = jax.ShapeDtypeStruct
    places = jnp.stack([core, x0, x1, slab])

    other_core, other_x0 = [(0, 1), (1, 0)], [(0, 1), (1, 0)]

    partner = lax.ppermute(integrals, ("x1", "x0"), [(0, 3), (3, 0), (1, 2), (2, 1)])

    steps = 4
    cut = pl.pallas_call(
        functools.partial(cut_body, steps),
        in_specs=[pl.BlockSpec(memory_space=pltpu.HBM)] * 2,
        out_specs=pl.BlockSpec(memory_space=pltpu.HBM),
        out_shape=shape((2 * zy, 8, LANES), BF16),
        scratch_shapes=[
            pltpu.SMEM(pair_irrep.shape, jnp.int32),
            pltpu.VMEM(amplitudes.shape, BF16),
            pltpu.VMEM((2 * zy, 8, LANES), BF16),
            pltpu.SemaphoreType.DMA,
            pltpu.SemaphoreType.DMA((steps,)),
            pltpu.SemaphoreType.DMA((steps,)),
        ],
        cost_estimate=pl.CostEstimate(flops=0, bytes_accessed=700000, transcendentals=0),
    )(pair_irrep, amplitudes)
    cut, block = lax.optimization_barrier((cut, integrals))
    mine = lax.all_to_all(
        cut.reshape(zy, 16, LANES), ("z", "y"), 0, 0, axis_index_groups=[ROLLED], tiled=True
    )
    ab_irrep = jnp.bitwise_xor(upper_irrep[:, None], virt_irrep[None, :])
    kept = (ab_irrep == cut[0, TILES, 0].astype(jnp.int32)).astype(F32)
    mine, kept = lax.optimization_barrier((mine, kept))
    mine = mine.reshape(zy, 2, 8, LANES)
    there = lax.ppermute(mine, "x0", other_x0)

    flat, wide = pltpu.VMEM((zy * 8, LANES), F32), pltpu.VMEM((zy, WIDE), F32)
    half, whole = shape((zy, NV), BF16), shape((2 * zy, NV), BF16)
    rows = call(
        functools.partial(rows_body, zy),
        [half, half, shape((zy, NV), F32)],
        "ssvvv",
        24000000 * 300,
        24000000,
        [flat, wide],
    )
    lhs, lhs2, sums = rows(places, slab_irrep, virt_irrep, mine, integrals)
    block2 = lax.ppermute(block, "core", other_core)
    partner, sums = lax.optimization_barrier((partner, sums))
    partner2 = lax.ppermute(partner, "core", other_core)
    after = call(
        functools.partial(there_body, zy),
        [whole, shape((2 * zy * 8, LANES), F32), shape((2 * zy, NV), F32)],
        "ssvvvvvvvv",
        40000000 * 300,
        40000000,
        [flat, wide, pltpu.VMEM((2 * zy, NV), BF16), pltpu.VMEM((2 * zy, NV), F32)],
    )
    rows2, own_sums, sums = after(
        places, slab_irrep, virt_irrep, there, lhs, lhs2, sums, integrals, block2, partner
    )
    ladder = call(
        functools.partial(ladder_body, zy), shape((2 * zy * 16, LANES), F32), "vvvv", 1000, 3000000
    )
    part = ladder(rows2, partner2, sums, own_sums)
    part = (part * SCALE).astype(F16).reshape(2 * zy, 16, LANES)
    back = lax.all_to_all(
        part, ("x0", "z", "y"), 0, 0, axis_index_groups=[ROLLED + [64 + i for i in ROLLED]], tiled=True
    )
    sums = jnp.sum(back.reshape(2, zy, 16, LANES).astype(F32), axis=1)
    finish = call(finish_body, shape((1, 4 * NV), BF16), "svvv", 0, 50000)
    return finish(places, sums, kept, residual_in)


def solution(mesh):
    fine = Mesh(mesh.devices.reshape(8, 8, 2, 2, 2), AXES)
    return jax.shard_map(
        per_device,
        mesh=fine,
        in_specs=(P(AXES, None), P(AXES[:3], AXES[3:]), P(AXES, None), P(AXES), P(), P(), P()),
        out_specs=P(AXES, None),
        check_vma=False,
    )
```

```python
import functools

import jax
import jax.numpy as jnp
from jax import lax
from jax.experimental import pallas as pl
from jax.experimental.pallas import tpu as pltpu
from jax.sharding import Mesh
from jax.sharding import PartitionSpec as P

AXES = ("z", "y", "core", "x1", "x0")
BF16, F32, F16 = jnp.bfloat16, jnp.float32, jnp.float16
NV = 800
LANES = 128
TILES = 7
WIDE = TILES * LANES
ROLLED = [(z + 4) % 8 * 8 + (y + 4) % 8 for z in range(8) for y in range(8)]
SCALE = 64.0

VMEM = pl.BlockSpec(memory_space=pltpu.VMEM)
SMEM = pl.BlockSpec(memory_space=pltpu.SMEM)


def call(body, out, ins, flops, nbytes, scratch=()):
    return pl.pallas_call(
        body,
        out_shape=out,
        in_specs=[SMEM if kind == "s" else VMEM for kind in ins],
        out_specs=jax.tree.map(lambda _: VMEM, out),
        scratch_shapes=list(scratch),
        compiler_params=pltpu.CompilerParams(vmem_limit_bytes=16 * 1024 * 1024),
        cost_estimate=pl.CostEstimate(flops=flops, bytes_accessed=nbytes, transcendentals=0),
    )


def cut_body(steps, pair_ref, row_ref, out_ref, pair, row, cut, pair_sem, in_sems, out_sems):
    lanes, slabs = row.shape[1] // steps, cut.shape[0] // steps

    def fetch(i):
        part = pl.ds(i * lanes, lanes)
        return pltpu.make_async_copy(row_ref.at[:, part], row.at[:, part], in_sems.at[i])

    def put(i):
        part = pl.ds(i * slabs, slabs)
        return pltpu.make_async_copy(cut.at[part], out_ref.at[part], out_sems.at[i])

    label = pltpu.make_async_copy(pair_ref, pair, pair_sem)
    label.start()

    def four(q, carry):
        for r in range(4):
            at = [pl.multiple_of(q * 3200 + (6 * r + t) * LANES, LANES) for t in range(TILES)]
            tiles = [row[:, pl.ds(a, LANES)].astype(F32) for a in at]
            chip = 2 * q + r // 2
            place = (chip // 8 + 4) % 8 * 8 + (chip + 4) % 8
            cut[2 * place + r % 2] = jnp.concatenate(tiles + [filler], axis=0).astype(BF16)
        return carry

    for i in range(steps):
        fetch(i).start()
    label.wait()
    filler = jnp.full((1, LANES), pair[0].astype(F32))
    for i in range(steps):
        fetch(i).wait()
        lax.fori_loop(i * slabs // 4, (i + 1) * slabs // 4, four, 0, unroll=4)
        put((i + 2) % 4).start()
    for i in range(steps):
        put(i).wait()


def put_tiles(sums, count, out_ref, first, step):
    wide = jnp.concatenate([sums, jnp.zeros((count, WIDE - NV), F32)], axis=1)
    for t in range(TILES):
        out_ref[pl.ds(first + t, count, stride=step), :] = wide[:, t * LANES : (t + 1) * LANES]


def kept_rows(flip, zy, places_ref, slab_ref, virt_ref, tiles_ref, flat, wide, lhs_ref, first):
    c = jnp.bitwise_xor(places_ref[3], flip)
    flat[...] = tiles_ref[:, jnp.bitwise_xor(places_ref[0], flip)].astype(F32).reshape(zy * 8, LANES)
    for t in range(TILES):
        wide[:, t * LANES : (t + 1) * LANES] = flat[pl.ds(t, zy, stride=8), :]
    pair = flat[pl.ds(TILES, zy, stride=8), :][:, 0:1]
    cd = jnp.bitwise_xor(virt_ref[...].reshape(1, NV), slab_ref[c]).astype(F32)
    for shift in range(4):

        @pl.when(c % 4 == shift)
        def _():
            row = wide[:, 32 * shift : 32 * shift + NV]
            lhs_ref[pl.ds(first, zy), :] = jnp.where(pair == cd, row, 0.0).astype(BF16)


def rows_body(zy, places_ref, slab_ref, virt_ref, tiles_ref, own_ref, lhs_ref, lhs2_ref, out_ref, flat, wide):
    kept_rows(0, zy, places_ref, slab_ref, virt_ref, tiles_ref, flat, wide, lhs_ref, 0)
    out_ref[...] = jnp.dot(lhs_ref[...], own_ref[...], preferred_element_type=F32)
    kept_rows(1, zy, places_ref, slab_ref, virt_ref, tiles_ref, flat, wide, lhs2_ref, 0)


def there_body(zy, *refs):
    places_ref, slab_ref, virt_ref, tiles_ref, lhs_ref, lhs2_ref, sums_ref = refs[:7]
    own_ref, own2_ref, block_ref = refs[7:10]
    rows2_ref, own_sums_ref, out_ref, flat, wide, rows, sums = refs[10:]
    here = pl.multiple_of(places_ref[1] * zy, zy)
    there = pl.multiple_of(zy - here, zy)
    rows[pl.ds(here, zy), :] = lhs_ref[...]
    rows2_ref[pl.ds(here, zy), :] = lhs2_ref[...]
    sums[pl.ds(here, zy), :] = sums_ref[...]
    kept_rows(0, zy, places_ref, slab_ref, virt_ref, tiles_ref, flat, wide, rows, there)
    kept_rows(1, zy, places_ref, slab_ref, virt_ref, tiles_ref, flat, wide, rows2_ref, there)
    own = jnp.dot(rows[pl.ds(there, zy), :], own_ref[...], preferred_element_type=F32)
    sums[pl.ds(there, zy), :] = own
    own = sums[...] + jnp.dot(rows2_ref[...], own2_ref[...], preferred_element_type=F32)
    put_tiles(own, 2 * zy, own_sums_ref, 0, TILES)
    out_ref[...] = jnp.dot(rows[...], block_ref[...], preferred_element_type=F32)


def ladder_body(zy, lhs_ref, block_ref, sums_ref, own_ref, out_ref):
    sums = sums_ref[...] + jnp.dot(lhs_ref[...], block_ref[...], preferred_element_type=F32)
    put_tiles(sums, 2 * zy, out_ref, TILES, 2 * TILES)
    for t in range(TILES):
        out_ref[pl.ds(t, 2 * zy, stride=2 * TILES), :] = own_ref[pl.ds(t, 2 * zy, stride=TILES), :]


def finish_body(places_ref, sums_ref, kept_ref, old_ref, out_ref):
    swap = places_ref[2] == 1
    order = ((0, 0), (1, 0), (1, 1), (0, 1))
    for a in range(4):
        (s, h), (s2, h2) = order[a], order[(a + 2) % 4]
        tiles = []
        for t in range(TILES):
            (p, q), (p2, q2) = divmod(TILES * h + t, 2), divmod(TILES * h2 + t, 2)
            tiles.append(jnp.where(swap, sums_ref[s2, p2, q2 : q2 + 1, :], sums_ref[s, p, q : q + 1, :]))
        row = jnp.concatenate(tiles, axis=1)[:, :NV] * (1.0 / SCALE)
        row = jnp.where(kept_ref[a : a + 1, :] > 0.5, row, 0.0)
        old = old_ref[:, a * NV : (a + 1) * NV].astype(F32)
        out_ref[:, a * NV : (a + 1) * NV] = (old + row).astype(BF16)


def per_device(amplitudes, integrals, residual_in, pair_irrep, slab_irrep, upper_irrep, virt_irrep):
    core = lax.axis_index("core")
    x1 = lax.axis_index("x1")
    x0 = lax.axis_index("x0")
    slab = lax.axis_index(("z", "y", "core"))
    zy = lax.axis_size("z") * lax.axis_size("y")
    shape = jax.ShapeDtypeStruct
    places = jnp.stack([core, x0, x1, slab])

    other_core, other_x0 = [(0, 1), (1, 0)], [(0, 1), (1, 0)]

    partner = lax.ppermute(integrals, ("x1", "x0"), [(0, 3), (3, 0), (1, 2), (2, 1)])

    steps = 4
    cut = pl.pallas_call(
        functools.partial(cut_body, steps),
        in_specs=[pl.BlockSpec(memory_space=pltpu.HBM)] * 2,
        out_specs=pl.BlockSpec(memory_space=pltpu.HBM),
        out_shape=shape((2 * zy, 8, LANES), BF16),
        scratch_shapes=[
            pltpu.SMEM(pair_irrep.shape, jnp.int32),
            pltpu.VMEM(amplitudes.shape, BF16),
            pltpu.VMEM((2 * zy, 8, LANES), BF16),
            pltpu.SemaphoreType.DMA,
            pltpu.SemaphoreType.DMA((steps,)),
            pltpu.SemaphoreType.DMA((steps,)),
        ],
        cost_estimate=pl.CostEstimate(flops=0, bytes_accessed=700000, transcendentals=0),
    )(pair_irrep, amplitudes)
    cut, block = lax.optimization_barrier((cut, integrals))
    mine = lax.all_to_all(
        cut.reshape(zy, 16, LANES), ("z", "y"), 0, 0, axis_index_groups=[ROLLED], tiled=True
    )
    ab_irrep = jnp.bitwise_xor(upper_irrep[:, None], virt_irrep[None, :])
    kept = (ab_irrep == cut[0, TILES, 0].astype(jnp.int32)).astype(F32)
    mine, kept = lax.optimization_barrier((mine, kept))
    mine = mine.reshape(zy, 2, 8, LANES)
    there = lax.ppermute(mine, "x0", other_x0)

    flat, wide = pltpu.VMEM((zy * 8, LANES), F32), pltpu.VMEM((zy, WIDE), F32)
    half, whole = shape((zy, NV), BF16), shape((2 * zy, NV), BF16)
    rows = call(
        functools.partial(rows_body, zy),
        [half, half, shape((zy, NV), F32)],
        "ssvvv",
        24000000 * 300,
        24000000,
        [flat, wide],
    )
    lhs, lhs2, sums = rows(places, slab_irrep, virt_irrep, mine, integrals)
    block2 = lax.ppermute(block, "core", other_core)
    partner, sums = lax.optimization_barrier((partner, sums))
    partner2 = lax.ppermute(partner, "core", other_core)
    after = call(
        functools.partial(there_body, zy),
        [whole, shape((2 * zy * TILES, LANES), F32), shape((2 * zy, NV), F32)],
        "ssvvvvvvvv",
        40000000 * 300,
        40000000,
        [flat, wide, pltpu.VMEM((2 * zy, NV), BF16), pltpu.VMEM((2 * zy, NV), F32)],
    )
    rows2, own_sums, sums = after(
        places, slab_irrep, virt_irrep, there, lhs, lhs2, sums, integrals, block2, partner
    )
    ladder = call(
        functools.partial(ladder_body, zy), shape((2 * zy * 2 * TILES, LANES), F32), "vvvv", 1000, 3000000
    )
    part = ladder(rows2, partner2, sums, own_sums)
    part = (part * SCALE).astype(F16).reshape(2 * zy, TILES, 2, LANES)
    back = lax.all_to_all(
        part, ("x0", "z", "y"), 0, 0, axis_index_groups=[ROLLED + [64 + i for i in ROLLED]], tiled=True
    )
    sums = jnp.sum(back.reshape(2, zy, TILES, 2, LANES).astype(F32), axis=1)
    finish = call(finish_body, shape((1, 4 * NV), BF16), "svvv", 0, 50000)
    return finish(places, sums, kept, residual_in)


def solution(mesh):
    fine = Mesh(mesh.devices.reshape(8, 8, 2, 2, 2), AXES)
    return jax.shard_map(
        per_device,
        mesh=fine,
        in_specs=(P(AXES, None), P(AXES[:3], AXES[3:]), P(AXES, None), P(AXES), P(), P(), P()),
        out_specs=P(AXES, None),
        check_vma=False,
    )
```

```python
import functools

import jax
import jax.numpy as jnp
from jax import lax
from jax.experimental import pallas as pl
from jax.experimental.pallas import tpu as pltpu
from jax.sharding import Mesh
from jax.sharding import PartitionSpec as P

AXES = ("z", "y", "core", "x1", "x0")
BF16, F32, F16 = jnp.bfloat16, jnp.float32, jnp.float16
NV = 800
LANES = 128
TILES = 7
WIDE = TILES * LANES
FIRST_Z = 7
ROLLED = [(z + FIRST_Z) % 8 * 8 + (y + 4) % 8 for z in range(8) for y in range(8)]
SCALE = 64.0

VMEM = pl.BlockSpec(memory_space=pltpu.VMEM)
SMEM = pl.BlockSpec(memory_space=pltpu.SMEM)


def call(body, out, ins, flops, nbytes, scratch=()):
    return pl.pallas_call(
        body,
        out_shape=out,
        in_specs=[SMEM if kind == "s" else VMEM for kind in ins],
        out_specs=jax.tree.map(lambda _: VMEM, out),
        scratch_shapes=list(scratch),
        compiler_params=pltpu.CompilerParams(vmem_limit_bytes=16 * 1024 * 1024),
        cost_estimate=pl.CostEstimate(flops=flops, bytes_accessed=nbytes, transcendentals=0),
    )


def cut_body(steps, pair_ref, row_ref, out_ref, pair, row, cut, pair_sem, in_sems, out_sems):
    lanes, slabs = row.shape[1] // steps, cut.shape[0] // steps
    rows = slabs // 2

    def fetch(i):
        part = pl.ds(i * lanes, lanes)
        return pltpu.make_async_copy(row_ref.at[:, part], row.at[:, part], in_sems.at[i])

    def put(z):
        part = cut.at[pl.ds(z * rows, rows)]
        return pltpu.make_async_copy(part, out_ref.at[pl.ds((z - FIRST_Z) % 8 * rows, rows)], out_sems.at[z])

    label = pltpu.make_async_copy(pair_ref, pair, pair_sem)
    label.start()

    def four(q, carry):
        for r in range(4):
            at = [pl.multiple_of(q * 3200 + (6 * r + t) * LANES, LANES) for t in range(TILES)]
            tiles = [row[:, pl.ds(a, LANES)].astype(F32) for a in at]
            cut[4 * jnp.bitwise_xor(q, 2) + r] = jnp.concatenate(tiles + [filler], axis=0).astype(BF16)
        return carry

    for i in range(steps):
        fetch(i).start()
    label.wait()
    filler = jnp.full((1, LANES), pair[0].astype(F32))
    for i in range(steps):
        fetch(i).wait()
        lax.fori_loop(i * slabs // 4, (i + 1) * slabs // 4, four, 0, unroll=4)
        put(2 * i).start()
        put(2 * i + 1).start()
    for z in range(2 * steps):
        put(z).wait()


def put_tiles(sums, count, out_ref, first, step):
    wide = jnp.concatenate([sums, jnp.zeros((count, WIDE - NV), F32)], axis=1)
    for t in range(TILES):
        out_ref[pl.ds(first + t, count, stride=step), :] = wide[:, t * LANES : (t + 1) * LANES]


def kept_rows(flip, zy, places_ref, slab_ref, virt_ref, tiles_ref, flat, wide, lhs_ref, first):
    c = jnp.bitwise_xor(places_ref[3], flip)
    flat[...] = tiles_ref[:, jnp.bitwise_xor(places_ref[0], flip)].astype(F32).reshape(zy * 8, LANES)
    for t in range(TILES):
        wide[:, t * LANES : (t + 1) * LANES] = flat[pl.ds(t, zy, stride=8), :]
    pair = flat[pl.ds(TILES, zy, stride=8), :][:, 0:1]
    cd = jnp.bitwise_xor(virt_ref[...].reshape(1, NV), slab_ref[c]).astype(F32)
    for shift in range(4):

        @pl.when(c % 4 == shift)
        def _():
            row = wide[:, 32 * shift : 32 * shift + NV]
            lhs_ref[pl.ds(first, zy), :] = jnp.where(pair == cd, row, 0.0).astype(BF16)


def rows_body(zy, places_ref, slab_ref, virt_ref, tiles_ref, own_ref, lhs_ref, lhs2_ref, out_ref, flat, wide):
    kept_rows(0, zy, places_ref, slab_ref, virt_ref, tiles_ref, flat, wide, lhs_ref, 0)
    out_ref[...] = jnp.dot(lhs_ref[...], own_ref[...], preferred_element_type=F32)
    kept_rows(1, zy, places_ref, slab_ref, virt_ref, tiles_ref, flat, wide, lhs2_ref, 0)


def there_body(zy, *refs):
    places_ref, slab_ref, virt_ref, tiles_ref, lhs_ref, lhs2_ref, sums_ref = refs[:7]
    own_ref, own2_ref, block_ref = refs[7:10]
    rows2_ref, own_sums_ref, out_ref, flat, wide, rows, sums = refs[10:]
    here = pl.multiple_of(places_ref[1] * zy, zy)
    there = pl.multiple_of(zy - here, zy)
    rows[pl.ds(here, zy), :] = lhs_ref[...]
    rows2_ref[pl.ds(here, zy), :] = lhs2_ref[...]
    sums[pl.ds(here, zy), :] = sums_ref[...]
    kept_rows(0, zy, places_ref, slab_ref, virt_ref, tiles_ref, flat, wide, rows, there)
    kept_rows(1, zy, places_ref, slab_ref, virt_ref, tiles_ref, flat, wide, rows2_ref, there)
    own = jnp.dot(rows[pl.ds(there, zy), :], own_ref[...], preferred_element_type=F32)
    sums[pl.ds(there, zy), :] = own
    own = sums[...] + jnp.dot(rows2_ref[...], own2_ref[...], preferred_element_type=F32)
    put_tiles(own, 2 * zy, own_sums_ref, 0, TILES)
    out_ref[...] = jnp.dot(rows[...], block_ref[...], preferred_element_type=F32)


def ladder_body(zy, lhs_ref, block_ref, sums_ref, own_ref, out_ref):
    sums = sums_ref[...] + jnp.dot(lhs_ref[...], block_ref[...], preferred_element_type=F32)
    put_tiles(sums, 2 * zy, out_ref, TILES, 2 * TILES)
    for t in range(TILES):
        out_ref[pl.ds(t, 2 * zy, stride=2 * TILES), :] = own_ref[pl.ds(t, 2 * zy, stride=TILES), :]


def finish_body(places_ref, sums_ref, kept_ref, old_ref, out_ref):
    swap = places_ref[2] == 1
    order = ((0, 0), (1, 0), (1, 1), (0, 1))
    for a in range(4):
        (s, h), (s2, h2) = order[a], order[(a + 2) % 4]
        tiles = []
        for t in range(TILES):
            (p, q), (p2, q2) = divmod(TILES * h + t, 2), divmod(TILES * h2 + t, 2)
            tiles.append(jnp.where(swap, sums_ref[s2, p2, q2 : q2 + 1, :], sums_ref[s, p, q : q + 1, :]))
        row = jnp.concatenate(tiles, axis=1)[:, :NV] * (1.0 / SCALE)
        row = jnp.where(kept_ref[a : a + 1, :] > 0.5, row, 0.0)
        old = old_ref[:, a * NV : (a + 1) * NV].astype(F32)
        out_ref[:, a * NV : (a + 1) * NV] = (old + row).astype(BF16)


def per_device(amplitudes, integrals, residual_in, pair_irrep, slab_irrep, upper_irrep, virt_irrep):
    core = lax.axis_index("core")
    x1 = lax.axis_index("x1")
    x0 = lax.axis_index("x0")
    slab = lax.axis_index(("z", "y", "core"))
    zy = lax.axis_size("z") * lax.axis_size("y")
    shape = jax.ShapeDtypeStruct
    places = jnp.stack([core, x0, x1, slab])

    other_core, other_x0 = [(0, 1), (1, 0)], [(0, 1), (1, 0)]

    partner = lax.ppermute(integrals, ("x1", "x0"), [(0, 3), (3, 0), (1, 2), (2, 1)])

    steps = 4
    cut = pl.pallas_call(
        functools.partial(cut_body, steps),
        in_specs=[pl.BlockSpec(memory_space=pltpu.HBM)] * 2,
        out_specs=pl.BlockSpec(memory_space=pltpu.HBM),
        out_shape=shape((2 * zy, 8, LANES), BF16),
        scratch_shapes=[
            pltpu.SMEM(pair_irrep.shape, jnp.int32),
            pltpu.VMEM(amplitudes.shape, BF16),
            pltpu.VMEM((2 * zy, 8, LANES), BF16),
            pltpu.SemaphoreType.DMA,
            pltpu.SemaphoreType.DMA((steps,)),
            pltpu.SemaphoreType.DMA((2 * steps,)),
        ],
        cost_estimate=pl.CostEstimate(flops=0, bytes_accessed=700000, transcendentals=0),
    )(pair_irrep, amplitudes)
    cut, block = lax.optimization_barrier((cut, integrals))
    mine = lax.all_to_all(
        cut.reshape(zy, 16, LANES), ("z", "y"), 0, 0, axis_index_groups=[ROLLED], tiled=True
    )
    ab_irrep = jnp.bitwise_xor(upper_irrep[:, None], virt_irrep[None, :])
    kept = (ab_irrep == cut[0, TILES, 0].astype(jnp.int32)).astype(F32)
    mine, kept = lax.optimization_barrier((mine, kept))
    mine = mine.reshape(zy, 2, 8, LANES)
    there = lax.ppermute(mine, "x0", other_x0)

    flat, wide = pltpu.VMEM((zy * 8, LANES), F32), pltpu.VMEM((zy, WIDE), F32)
    half, whole = shape((zy, NV), BF16), shape((2 * zy, NV), BF16)
    rows = call(
        functools.partial(rows_body, zy),
        [half, half, shape((zy, NV), F32)],
        "ssvvv",
        24000000 * 300,
        24000000,
        [flat, wide],
    )
    lhs, lhs2, sums = rows(places, slab_irrep, virt_irrep, mine, integrals)
    block2 = lax.ppermute(block, "core", other_core)
    partner, sums = lax.optimization_barrier((partner, sums))
    partner2 = lax.ppermute(partner, "core", other_core)
    after = call(
        functools.partial(there_body, zy),
        [whole, shape((2 * zy * TILES, LANES), F32), shape((2 * zy, NV), F32)],
        "ssvvvvvvvv",
        40000000 * 300,
        40000000,
        [flat, wide, pltpu.VMEM((2 * zy, NV), BF16), pltpu.VMEM((2 * zy, NV), F32)],
    )
    rows2, own_sums, sums = after(
        places, slab_irrep, virt_irrep, there, lhs, lhs2, sums, integrals, block2, partner
    )
    ladder = call(
        functools.partial(ladder_body, zy), shape((2 * zy * 2 * TILES, LANES), F32), "vvvv", 1000, 3000000
    )
    part = ladder(rows2, partner2, sums, own_sums)
    part = (part * SCALE).astype(F16).reshape(2 * zy, TILES, 2, LANES)
    back = lax.all_to_all(
        part, ("x0", "z", "y"), 0, 0, axis_index_groups=[ROLLED + [64 + i for i in ROLLED]], tiled=True
    )
    sums = jnp.sum(back.reshape(2, zy, TILES, 2, LANES).astype(F32), axis=1)
    finish = call(finish_body, shape((1, 4 * NV), BF16), "svvv", 0, 50000)
    return finish(places, sums, kept, residual_in)


def solution(mesh):
    fine = Mesh(mesh.devices.reshape(8, 8, 2, 2, 2), AXES)
    return jax.shard_map(
        per_device,
        mesh=fine,
        in_specs=(P(AXES, None), P(AXES[:3], AXES[3:]), P(AXES, None), P(AXES), P(), P(), P()),
        out_specs=P(AXES, None),
        check_vma=False,
    )
```

```python
import functools

import jax
import jax.numpy as jnp
from jax import lax
from jax.experimental import pallas as pl
from jax.experimental.pallas import tpu as pltpu
from jax.sharding import Mesh
from jax.sharding import PartitionSpec as P

AXES = ("z", "y", "core", "x1", "x0")
BF16, F32, F16 = jnp.bfloat16, jnp.float32, jnp.float16
NV = 800
LANES = 128
TILES = 7
WIDE = TILES * LANES
FIRST_Z = 4
ROLLED = [(z + FIRST_Z) % 8 * 8 + (y + 4) % 8 for z in range(8) for y in range(8)]
SCALE = 64.0

VMEM = pl.BlockSpec(memory_space=pltpu.VMEM)
SMEM = pl.BlockSpec(memory_space=pltpu.SMEM)


def call(body, out, ins, flops, nbytes, scratch=()):
    return pl.pallas_call(
        body,
        out_shape=out,
        in_specs=[SMEM if kind == "s" else VMEM for kind in ins],
        out_specs=jax.tree.map(lambda _: VMEM, out),
        scratch_shapes=list(scratch),
        compiler_params=pltpu.CompilerParams(vmem_limit_bytes=16 * 1024 * 1024),
        cost_estimate=pl.CostEstimate(flops=flops, bytes_accessed=nbytes, transcendentals=0),
    )


def cut_body(steps, pair_ref, row_ref, out_ref, pair, row, cut, pair_sem, in_sems, out_sems):
    lanes, slabs = row.shape[1] // steps, cut.shape[0] // steps
    rows = slabs // 2

    def fetch(i):
        part = pl.ds(i * lanes, lanes)
        return pltpu.make_async_copy(row_ref.at[:, part], row.at[:, part], in_sems.at[i])

    def put(z):
        part = cut.at[pl.ds(z * rows, rows)]
        return pltpu.make_async_copy(part, out_ref.at[pl.ds((z - FIRST_Z) % 8 * rows, rows)], out_sems.at[z])

    label = pltpu.make_async_copy(pair_ref, pair, pair_sem)
    label.start()

    def four(q, carry):
        for r in range(4):
            at = [pl.multiple_of(q * 3200 + (6 * r + t) * LANES, LANES) for t in range(TILES)]
            tiles = [row[:, pl.ds(a, LANES)].astype(F32) for a in at]
            cut[4 * jnp.bitwise_xor(q, 2) + r] = jnp.concatenate(tiles + [filler], axis=0).astype(BF16)
        return carry

    for i in range(steps):
        fetch(i).start()
    label.wait()
    filler = jnp.full((1, LANES), pair[0].astype(F32))
    for i in range(steps):
        fetch(i).wait()
        lax.fori_loop(i * slabs // 4, (i + 1) * slabs // 4, four, 0, unroll=4)
        put(2 * i).start()
        put(2 * i + 1).start()
    for z in range(2 * steps):
        put(z).wait()


def put_tiles(sums, count, out_ref, first, step):
    wide = jnp.concatenate([sums, jnp.zeros((count, WIDE - NV), F32)], axis=1)
    for t in range(TILES):
        out_ref[pl.ds(first + t, count, stride=step), :] = wide[:, t * LANES : (t + 1) * LANES]


def kept_rows(flip, zy, places_ref, slab_ref, virt_ref, tiles_ref, flat, wide, lhs_ref, first):
    c = jnp.bitwise_xor(places_ref[3], flip)
    flat[...] = tiles_ref[:, jnp.bitwise_xor(places_ref[0], flip)].astype(F32).reshape(zy * 8, LANES)
    for t in range(TILES):
        wide[:, t * LANES : (t + 1) * LANES] = flat[pl.ds(t, zy, stride=8), :]
    pair = flat[pl.ds(TILES, zy, stride=8), :][:, 0:1]
    cd = jnp.bitwise_xor(virt_ref[...].reshape(1, NV), slab_ref[c]).astype(F32)
    for shift in range(4):

        @pl.when(c % 4 == shift)
        def _():
            row = wide[:, 32 * shift : 32 * shift + NV]
            lhs_ref[pl.ds(first, zy), :] = jnp.where(pair == cd, row, 0.0).astype(BF16)


def rows_body(zy, places_ref, slab_ref, virt_ref, tiles_ref, own_ref, lhs_ref, lhs2_ref, out_ref, flat, wide):
    kept_rows(0, zy, places_ref, slab_ref, virt_ref, tiles_ref, flat, wide, lhs_ref, 0)
    out_ref[...] = jnp.dot(lhs_ref[...], own_ref[...], preferred_element_type=F32)
    kept_rows(1, zy, places_ref, slab_ref, virt_ref, tiles_ref, flat, wide, lhs2_ref, 0)


def there_body(zy, *refs):
    places_ref, slab_ref, virt_ref, tiles_ref, lhs_ref, lhs2_ref, sums_ref = refs[:7]
    own_ref, own2_ref, block_ref = refs[7:10]
    rows2_ref, own_sums_ref, out_ref, flat, wide, rows, sums = refs[10:]
    here = pl.multiple_of(places_ref[1] * zy, zy)
    there = pl.multiple_of(zy - here, zy)
    rows[pl.ds(here, zy), :] = lhs_ref[...]
    rows2_ref[pl.ds(here, zy), :] = lhs2_ref[...]
    sums[pl.ds(here, zy), :] = sums_ref[...]
    kept_rows(0, zy, places_ref, slab_ref, virt_ref, tiles_ref, flat, wide, rows, there)
    kept_rows(1, zy, places_ref, slab_ref, virt_ref, tiles_ref, flat, wide, rows2_ref, there)
    own = jnp.dot(rows[pl.ds(there, zy), :], own_ref[...], preferred_element_type=F32)
    sums[pl.ds(there, zy), :] = own
    own = sums[...] + jnp.dot(rows2_ref[...], own2_ref[...], preferred_element_type=F32)
    put_tiles(own, 2 * zy, own_sums_ref, 0, TILES)
    out_ref[...] = jnp.dot(rows[...], block_ref[...], preferred_element_type=F32)


def ladder_body(zy, lhs_ref, block_ref, sums_ref, own_ref, out_ref):
    sums = sums_ref[...] + jnp.dot(lhs_ref[...], block_ref[...], preferred_element_type=F32)
    put_tiles(sums, 2 * zy, out_ref, TILES, 2 * TILES)
    for t in range(TILES):
        out_ref[pl.ds(t, 2 * zy, stride=2 * TILES), :] = own_ref[pl.ds(t, 2 * zy, stride=TILES), :]


def finish_body(places_ref, sums_ref, kept_ref, old_ref, out_ref):
    swap = places_ref[2] == 1
    order = ((0, 0), (1, 0), (1, 1), (0, 1))
    for a in range(4):
        (s, h), (s2, h2) = order[a], order[(a + 2) % 4]
        tiles = []
        for t in range(TILES):
            (p, q), (p2, q2) = divmod(TILES * h + t, 2), divmod(TILES * h2 + t, 2)
            tiles.append(jnp.where(swap, sums_ref[s2, p2, q2 : q2 + 1, :], sums_ref[s, p, q : q + 1, :]))
        row = jnp.concatenate(tiles, axis=1)[:, :NV] * (1.0 / SCALE)
        row = jnp.where(kept_ref[a : a + 1, :] > 0.5, row, 0.0)
        old = old_ref[:, a * NV : (a + 1) * NV].astype(F32)
        out_ref[:, a * NV : (a + 1) * NV] = (old + row).astype(BF16)


def per_device(amplitudes, integrals, residual_in, pair_irrep, slab_irrep, upper_irrep, virt_irrep):
    core = lax.axis_index("core")
    x1 = lax.axis_index("x1")
    x0 = lax.axis_index("x0")
    slab = lax.axis_index(("z", "y", "core"))
    zy = lax.axis_size("z") * lax.axis_size("y")
    shape = jax.ShapeDtypeStruct
    places = jnp.stack([core, x0, x1, slab])

    other_core, other_x0 = [(0, 1), (1, 0)], [(0, 1), (1, 0)]

    partner = lax.ppermute(integrals, ("x1", "x0"), [(0, 3), (3, 0), (1, 2), (2, 1)])

    steps = 4
    cut = pl.pallas_call(
        functools.partial(cut_body, steps),
        in_specs=[pl.BlockSpec(memory_space=pltpu.HBM)] * 2,
        out_specs=pl.BlockSpec(memory_space=pltpu.HBM),
        out_shape=shape((2 * zy, 8, LANES), BF16),
        scratch_shapes=[
            pltpu.SMEM(pair_irrep.shape, jnp.int32),
            pltpu.VMEM(amplitudes.shape, BF16),
            pltpu.VMEM((2 * zy, 8, LANES), BF16),
            pltpu.SemaphoreType.DMA,
            pltpu.SemaphoreType.DMA((steps,)),
            pltpu.SemaphoreType.DMA((2 * steps,)),
        ],
        cost_estimate=pl.CostEstimate(flops=0, bytes_accessed=700000, transcendentals=0),
    )(pair_irrep, amplitudes)
    cut, block = lax.optimization_barrier((cut, integrals))
    mine = lax.all_to_all(
        cut.reshape(zy, 16, LANES), ("z", "y"), 0, 0, axis_index_groups=[ROLLED], tiled=True
    )
    ab_irrep = jnp.bitwise_xor(upper_irrep[:, None], virt_irrep[None, :])
    kept = (ab_irrep == cut[0, TILES, 0].astype(jnp.int32)).astype(F32)
    mine, kept = lax.optimization_barrier((mine, kept))
    mine = mine.reshape(zy, 2, 8, LANES)
    there = lax.ppermute(mine, "x0", other_x0)

    flat, wide = pltpu.VMEM((zy * 8, LANES), F32), pltpu.VMEM((zy, WIDE), F32)
    half, whole = shape((zy, NV), BF16), shape((2 * zy, NV), BF16)
    rows = call(
        functools.partial(rows_body, zy),
        [half, half, shape((zy, NV), F32)],
        "ssvvv",
        24000000 * 300,
        24000000,
        [flat, wide],
    )
    lhs, lhs2, sums = rows(places, slab_irrep, virt_irrep, mine, integrals)
    block2 = lax.ppermute(block, "core", other_core)
    partner, sums = lax.optimization_barrier((partner, sums))
    partner2 = lax.ppermute(partner, "core", other_core)
    after = call(
        functools.partial(there_body, zy),
        [whole, shape((2 * zy * TILES, LANES), F32), shape((2 * zy, NV), F32)],
        "ssvvvvvvvv",
        40000000 * 300,
        40000000,
        [flat, wide, pltpu.VMEM((2 * zy, NV), BF16), pltpu.VMEM((2 * zy, NV), F32)],
    )
    rows2, own_sums, sums = after(
        places, slab_irrep, virt_irrep, there, lhs, lhs2, sums, integrals, block2, partner
    )
    ladder = call(
        functools.partial(ladder_body, zy), shape((2 * zy * 2 * TILES, LANES), F32), "vvvv", 1000, 3000000
    )
    part = ladder(rows2, partner2, sums, own_sums)
    part = (part * SCALE).astype(F16).reshape(2 * zy, TILES, 2, LANES)
    back = lax.all_to_all(
        part, ("x0", "z", "y"), 0, 0, axis_index_groups=[ROLLED + [64 + i for i in ROLLED]], tiled=True
    )
    sums = jnp.sum(back.reshape(2, zy, TILES, 2, LANES).astype(F32), axis=1)
    finish = call(finish_body, shape((1, 4 * NV), BF16), "svvv", 0, 50000)
    return finish(places, sums, kept, residual_in)


def solution(mesh):
    fine = Mesh(mesh.devices.reshape(8, 8, 2, 2, 2), AXES)
    return jax.shard_map(
        per_device,
        mesh=fine,
        in_specs=(P(AXES, None), P(AXES[:3], AXES[3:]), P(AXES, None), P(AXES), P(), P(), P()),
        out_specs=P(AXES, None),
        check_vma=False,
    )
```

```python
import functools

import jax
import jax.numpy as jnp
from jax import lax
from jax.experimental import pallas as pl
from jax.experimental.pallas import tpu as pltpu
from jax.sharding import Mesh
from jax.sharding import PartitionSpec as P

AXES = ("z", "y", "core", "x1", "x0")
BF16, F32, F16 = jnp.bfloat16, jnp.float32, jnp.float16
NV = 800
LANES = 128
TILES = 7
WIDE = TILES * LANES
ORDER_Z = (4, 0, 1, 2, 3, 5, 6, 7)
ROLLED = [z * 8 + (y + 4) % 8 for z in ORDER_Z for y in range(8)]
SCALE = 64.0

VMEM = pl.BlockSpec(memory_space=pltpu.VMEM)
SMEM = pl.BlockSpec(memory_space=pltpu.SMEM)


def call(body, out, ins, flops, nbytes, scratch=()):
    return pl.pallas_call(
        body,
        out_shape=out,
        in_specs=[SMEM if kind == "s" else VMEM for kind in ins],
        out_specs=jax.tree.map(lambda _: VMEM, out),
        scratch_shapes=list(scratch),
        compiler_params=pltpu.CompilerParams(vmem_limit_bytes=16 * 1024 * 1024),
        cost_estimate=pl.CostEstimate(flops=flops, bytes_accessed=nbytes, transcendentals=0),
    )


def cut_body(steps, pair_ref, row_ref, out_ref, pair, row, cut, pair_sem, in_sems, out_sems):
    lanes, slabs = row.shape[1] // steps, cut.shape[0] // steps
    rows = slabs // 2

    def fetch(i):
        part = pl.ds(i * lanes, lanes)
        return pltpu.make_async_copy(row_ref.at[:, part], row.at[:, part], in_sems.at[i])

    def put(z):
        part = cut.at[pl.ds(z * rows, rows)]
        return pltpu.make_async_copy(part, out_ref.at[pl.ds(ORDER_Z.index(z) * rows, rows)], out_sems.at[z])

    label = pltpu.make_async_copy(pair_ref, pair, pair_sem)
    label.start()

    def four(q, carry):
        for r in range(4):
            at = [pl.multiple_of(q * 3200 + (6 * r + t) * LANES, LANES) for t in range(TILES)]
            tiles = [row[:, pl.ds(a, LANES)].astype(F32) for a in at]
            cut[4 * jnp.bitwise_xor(q, 2) + r] = jnp.concatenate(tiles + [filler], axis=0).astype(BF16)
        return carry

    for i in range(steps):
        fetch(i).start()
    label.wait()
    filler = jnp.full((1, LANES), pair[0].astype(F32))
    for i in range(steps):
        fetch(i).wait()
        lax.fori_loop(i * slabs // 4, (i + 1) * slabs // 4, four, 0, unroll=4)
        put(2 * i).start()
        put(2 * i + 1).start()
    for z in range(2 * steps):
        put(z).wait()


def put_tiles(sums, count, out_ref, first, step):
    wide = jnp.concatenate([sums, jnp.zeros((count, WIDE - NV), F32)], axis=1)
    for t in range(TILES):
        out_ref[pl.ds(first + t, count, stride=step), :] = wide[:, t * LANES : (t + 1) * LANES]


def kept_rows(flip, zy, places_ref, slab_ref, virt_ref, tiles_ref, flat, wide, lhs_ref, first):
    c = jnp.bitwise_xor(places_ref[3], flip)
    flat[...] = tiles_ref[:, jnp.bitwise_xor(places_ref[0], flip)].astype(F32).reshape(zy * 8, LANES)
    for t in range(TILES):
        wide[:, t * LANES : (t + 1) * LANES] = flat[pl.ds(t, zy, stride=8), :]
    pair = flat[pl.ds(TILES, zy, stride=8), :][:, 0:1]
    cd = jnp.bitwise_xor(virt_ref[...].reshape(1, NV), slab_ref[c]).astype(F32)
    for shift in range(4):

        @pl.when(c % 4 == shift)
        def _():
            row = wide[:, 32 * shift : 32 * shift + NV]
            lhs_ref[pl.ds(first, zy), :] = jnp.where(pair == cd, row, 0.0).astype(BF16)


def rows_body(zy, places_ref, slab_ref, virt_ref, tiles_ref, own_ref, lhs_ref, lhs2_ref, out_ref, flat, wide):
    kept_rows(0, zy, places_ref, slab_ref, virt_ref, tiles_ref, flat, wide, lhs_ref, 0)
    out_ref[...] = jnp.dot(lhs_ref[...], own_ref[...], preferred_element_type=F32)
    kept_rows(1, zy, places_ref, slab_ref, virt_ref, tiles_ref, flat, wide, lhs2_ref, 0)


def there_body(zy, *refs):
    places_ref, slab_ref, virt_ref, tiles_ref, lhs_ref, lhs2_ref, sums_ref = refs[:7]
    own_ref, own2_ref, block_ref = refs[7:10]
    rows2_ref, own_sums_ref, out_ref, flat, wide, rows, sums = refs[10:]
    here = pl.multiple_of(places_ref[1] * zy, zy)
    there = pl.multiple_of(zy - here, zy)
    rows[pl.ds(here, zy), :] = lhs_ref[...]
    rows2_ref[pl.ds(here, zy), :] = lhs2_ref[...]
    sums[pl.ds(here, zy), :] = sums_ref[...]
    kept_rows(0, zy, places_ref, slab_ref, virt_ref, tiles_ref, flat, wide, rows, there)
    kept_rows(1, zy, places_ref, slab_ref, virt_ref, tiles_ref, flat, wide, rows2_ref, there)
    own = jnp.dot(rows[pl.ds(there, zy), :], own_ref[...], preferred_element_type=F32)
    sums[pl.ds(there, zy), :] = own
    own = sums[...] + jnp.dot(rows2_ref[...], own2_ref[...], preferred_element_type=F32)
    put_tiles(own, 2 * zy, own_sums_ref, 0, TILES)
    out_ref[...] = jnp.dot(rows[...], block_ref[...], preferred_element_type=F32)


def ladder_body(zy, lhs_ref, block_ref, sums_ref, own_ref, out_ref):
    sums = sums_ref[...] + jnp.dot(lhs_ref[...], block_ref[...], preferred_element_type=F32)
    put_tiles(sums, 2 * zy, out_ref, TILES, 2 * TILES)
    for t in range(TILES):
        out_ref[pl.ds(t, 2 * zy, stride=2 * TILES), :] = own_ref[pl.ds(t, 2 * zy, stride=TILES), :]


def finish_body(places_ref, sums_ref, kept_ref, old_ref, out_ref):
    swap = places_ref[2] == 1
    order = ((0, 0), (1, 0), (1, 1), (0, 1))
    for a in range(4):
        (s, h), (s2, h2) = order[a], order[(a + 2) % 4]
        tiles = []
        for t in range(TILES):
            (p, q), (p2, q2) = divmod(TILES * h + t, 2), divmod(TILES * h2 + t, 2)
            tiles.append(jnp.where(swap, sums_ref[s2, p2, q2 : q2 + 1, :], sums_ref[s, p, q : q + 1, :]))
        row = jnp.concatenate(tiles, axis=1)[:, :NV] * (1.0 / SCALE)
        row = jnp.where(kept_ref[a : a + 1, :] > 0.5, row, 0.0)
        old = old_ref[:, a * NV : (a + 1) * NV].astype(F32)
        out_ref[:, a * NV : (a + 1) * NV] = (old + row).astype(BF16)


def per_device(amplitudes, integrals, residual_in, pair_irrep, slab_irrep, upper_irrep, virt_irrep):
    core = lax.axis_index("core")
    x1 = lax.axis_index("x1")
    x0 = lax.axis_index("x0")
    slab = lax.axis_index(("z", "y", "core"))
    zy = lax.axis_size("z") * lax.axis_size("y")
    shape = jax.ShapeDtypeStruct
    places = jnp.stack([core, x0, x1, slab])

    other_core, other_x0 = [(0, 1), (1, 0)], [(0, 1), (1, 0)]

    partner = lax.ppermute(integrals, ("x1", "x0"), [(0, 3), (3, 0), (1, 2), (2, 1)])

    steps = 4
    cut = pl.pallas_call(
        functools.partial(cut_body, steps),
        in_specs=[pl.BlockSpec(memory_space=pltpu.HBM)] * 2,
        out_specs=pl.BlockSpec(memory_space=pltpu.HBM),
        out_shape=shape((2 * zy, 8, LANES), BF16),
        scratch_shapes=[
            pltpu.SMEM(pair_irrep.shape, jnp.int32),
            pltpu.VMEM(amplitudes.shape, BF16),
            pltpu.VMEM((2 * zy, 8, LANES), BF16),
            pltpu.SemaphoreType.DMA,
            pltpu.SemaphoreType.DMA((steps,)),
            pltpu.SemaphoreType.DMA((2 * steps,)),
        ],
        cost_estimate=pl.CostEstimate(flops=0, bytes_accessed=700000, transcendentals=0),
    )(pair_irrep, amplitudes)
    cut, block = lax.optimization_barrier((cut, integrals))
    mine = lax.all_to_all(
        cut.reshape(zy, 16, LANES), ("z", "y"), 0, 0, axis_index_groups=[ROLLED], tiled=True
    )
    ab_irrep = jnp.bitwise_xor(upper_irrep[:, None], virt_irrep[None, :])
    kept = (ab_irrep == cut[0, TILES, 0].astype(jnp.int32)).astype(F32)
    mine, kept = lax.optimization_barrier((mine, kept))
    mine = mine.reshape(zy, 2, 8, LANES)
    there = lax.ppermute(mine, "x0", other_x0)

    flat, wide = pltpu.VMEM((zy * 8, LANES), F32), pltpu.VMEM((zy, WIDE), F32)
    half, whole = shape((zy, NV), BF16), shape((2 * zy, NV), BF16)
    rows = call(
        functools.partial(rows_body, zy),
        [half, half, shape((zy, NV), F32)],
        "ssvvv",
        24000000 * 300,
        24000000,
        [flat, wide],
    )
    lhs, lhs2, sums = rows(places, slab_irrep, virt_irrep, mine, integrals)
    block2 = lax.ppermute(block, "core", other_core)
    partner, sums = lax.optimization_barrier((partner, sums))
    partner2 = lax.ppermute(partner, "core", other_core)
    after = call(
        functools.partial(there_body, zy),
        [whole, shape((2 * zy * TILES, LANES), F32), shape((2 * zy, NV), F32)],
        "ssvvvvvvvv",
        40000000 * 300,
        40000000,
        [flat, wide, pltpu.VMEM((2 * zy, NV), BF16), pltpu.VMEM((2 * zy, NV), F32)],
    )
    rows2, own_sums, sums = after(
        places, slab_irrep, virt_irrep, there, lhs, lhs2, sums, integrals, block2, partner
    )
    ladder = call(
        functools.partial(ladder_body, zy), shape((2 * zy * 2 * TILES, LANES), F32), "vvvv", 1000, 3000000
    )
    part = ladder(rows2, partner2, sums, own_sums)
    part = (part * SCALE).astype(F16).reshape(2 * zy, TILES, 2, LANES)
    back = lax.all_to_all(
        part, ("x0", "z", "y"), 0, 0, axis_index_groups=[ROLLED + [64 + i for i in ROLLED]], tiled=True
    )
    sums = jnp.sum(back.reshape(2, zy, TILES, 2, LANES).astype(F32), axis=1)
    finish = call(finish_body, shape((1, 4 * NV), BF16), "svvv", 0, 50000)
    return finish(places, sums, kept, residual_in)


def solution(mesh):
    fine = Mesh(mesh.devices.reshape(8, 8, 2, 2, 2), AXES)
    return jax.shard_map(
        per_device,
        mesh=fine,
        in_specs=(P(AXES, None), P(AXES[:3], AXES[3:]), P(AXES, None), P(AXES), P(), P(), P()),
        out_specs=P(AXES, None),
        check_vma=False,
    )
```

```python
import functools

import jax
import jax.numpy as jnp
from jax import lax
from jax.experimental import pallas as pl
from jax.experimental.pallas import tpu as pltpu
from jax.sharding import Mesh
from jax.sharding import PartitionSpec as P

AXES = ("z", "y", "core", "x1", "x0")
BF16, F32, F16 = jnp.bfloat16, jnp.float32, jnp.float16
NV = 800
LANES = 128
TILES = 7
WIDE = TILES * LANES
ORDER_Z = (4, 0, 1, 2, 3, 5, 6, 7)
ROLLED = [z * 8 + (y + 4) % 8 for z in ORDER_Z for y in range(8)]
SCALE = 64.0

VMEM = pl.BlockSpec(memory_space=pltpu.VMEM)
SMEM = pl.BlockSpec(memory_space=pltpu.SMEM)


def call(body, out, ins, flops, nbytes, scratch=()):
    return pl.pallas_call(
        body,
        out_shape=out,
        in_specs=[SMEM if kind == "s" else VMEM for kind in ins],
        out_specs=jax.tree.map(lambda _: VMEM, out),
        scratch_shapes=list(scratch),
        compiler_params=pltpu.CompilerParams(vmem_limit_bytes=16 * 1024 * 1024),
        cost_estimate=pl.CostEstimate(flops=flops, bytes_accessed=nbytes, transcendentals=0),
    )


def cut_body(steps, pair_ref, row_ref, out_ref, pair, row, cut, pair_sem, in_sems, out_sems):
    lanes, slabs = row.shape[1] // steps, cut.shape[0] // steps
    rows = slabs // 2

    def fetch(i):
        part = pl.ds(i * lanes, lanes)
        return pltpu.make_async_copy(row_ref.at[:, part], row.at[:, part], in_sems.at[i])

    def put(z):
        part = cut.at[pl.ds(z * rows, rows)]
        return pltpu.make_async_copy(part, out_ref.at[pl.ds(ORDER_Z.index(z) * rows, rows)], out_sems.at[z])

    label = pltpu.make_async_copy(pair_ref, pair, pair_sem)
    label.start()

    def four(q, carry):
        for r in range(4):
            at = [pl.multiple_of(q * 3200 + (6 * r + t) * LANES, LANES) for t in range(TILES)]
            tiles = [row[:, pl.ds(a, LANES)].astype(F32) for a in at]
            cut[4 * jnp.bitwise_xor(q, 2) + r] = jnp.concatenate(tiles + [filler], axis=0).astype(BF16)
        return carry

    for i in range(steps):
        fetch(i).start()
    label.wait()
    filler = jnp.full((1, LANES), pair[0].astype(F32))
    for i in range(steps):
        fetch(i).wait()
        lax.fori_loop(i * slabs // 4, (i + 1) * slabs // 4, four, 0, unroll=4)
        put(2 * i).start()
        put(2 * i + 1).start()
    for z in range(2 * steps):
        put(z).wait()


def put_tiles(sums, count, out_ref, first, step):
    wide = jnp.concatenate([sums, jnp.zeros((count, WIDE - NV), F32)], axis=1)
    for t in range(TILES):
        out_ref[pl.ds(first + t, count, stride=step), :] = wide[:, t * LANES : (t + 1) * LANES]


def kept_rows(flip, zy, places_ref, slab_ref, virt_ref, tiles_ref, flat, wide, lhs_ref, first):
    c = jnp.bitwise_xor(places_ref[3], flip)
    flat[...] = tiles_ref[:, jnp.bitwise_xor(places_ref[0], flip)].astype(F32).reshape(zy * 8, LANES)
    for t in range(TILES):
        wide[:, t * LANES : (t + 1) * LANES] = flat[pl.ds(t, zy, stride=8), :]
    pair = flat[pl.ds(TILES, zy, stride=8), :][:, 0:1]
    cd = jnp.bitwise_xor(virt_ref[...].reshape(1, NV), slab_ref[c]).astype(F32)
    for shift in range(4):

        @pl.when(c % 4 == shift)
        def _():
            row = wide[:, 32 * shift : 32 * shift + NV]
            lhs_ref[pl.ds(first, zy), :] = jnp.where(pair == cd, row, 0.0).astype(BF16)


def rows_body(zy, places_ref, slab_ref, virt_ref, tiles_ref, own_ref, lhs_ref, lhs2_ref, out_ref, flat, wide):
    kept_rows(0, zy, places_ref, slab_ref, virt_ref, tiles_ref, flat, wide, lhs_ref, 0)
    out_ref[...] = jnp.dot(lhs_ref[...], own_ref[...], preferred_element_type=F32)
    kept_rows(1, zy, places_ref, slab_ref, virt_ref, tiles_ref, flat, wide, lhs2_ref, 0)


def there_body(zy, *refs):
    places_ref, slab_ref, virt_ref, tiles_ref, lhs_ref, lhs2_ref, sums_ref = refs[:7]
    own_ref, own2_ref, block_ref = refs[7:10]
    rows2_ref, own_sums_ref, out_ref, flat, wide, rows, sums = refs[10:]
    here = pl.multiple_of(places_ref[1] * zy, zy)
    there = pl.multiple_of(zy - here, zy)
    rows[pl.ds(here, zy), :] = lhs_ref[...]
    rows2_ref[pl.ds(here, zy), :] = lhs2_ref[...]
    sums[pl.ds(here, zy), :] = sums_ref[...]
    kept_rows(0, zy, places_ref, slab_ref, virt_ref, tiles_ref, flat, wide, rows, there)
    kept_rows(1, zy, places_ref, slab_ref, virt_ref, tiles_ref, flat, wide, rows2_ref, there)
    own = jnp.dot(rows[pl.ds(there, zy), :], own_ref[...], preferred_element_type=F32)
    sums[pl.ds(there, zy), :] = own
    own = sums[...] + jnp.dot(rows2_ref[...], own2_ref[...], preferred_element_type=F32)
    put_tiles(own, 2 * zy, own_sums_ref, 0, TILES)
    out_ref[...] = jnp.dot(rows[...], block_ref[...], preferred_element_type=F32)


def ladder_body(zy, lhs_ref, block_ref, sums_ref, own_ref, out_ref):
    sums = sums_ref[...] + jnp.dot(lhs_ref[...], block_ref[...], preferred_element_type=F32)
    put_tiles(sums, 2 * zy, out_ref, TILES, 2 * TILES)
    for t in range(TILES):
        out_ref[pl.ds(t, 2 * zy, stride=2 * TILES), :] = own_ref[pl.ds(t, 2 * zy, stride=TILES), :]


def finish_body(sums_ref, kept_ref, old_ref, out_ref):
    swap = kept_ref[4:5, 0:LANES] > 0.5
    order = ((0, 0), (1, 0), (1, 1), (0, 1))
    for a in range(4):
        (s, h), (s2, h2) = order[a], order[(a + 2) % 4]
        tiles = []
        for t in range(TILES):
            (p, q), (p2, q2) = divmod(TILES * h + t, 2), divmod(TILES * h2 + t, 2)
            tiles.append(jnp.where(swap, sums_ref[s2, p2, q2 : q2 + 1, :], sums_ref[s, p, q : q + 1, :]))
        row = jnp.concatenate(tiles, axis=1)[:, :NV] * (1.0 / SCALE)
        row = jnp.where(kept_ref[a : a + 1, :] > 0.5, row, 0.0)
        old = old_ref[:, a * NV : (a + 1) * NV].astype(F32)
        out_ref[:, a * NV : (a + 1) * NV] = (old + row).astype(BF16)


def per_device(amplitudes, integrals, residual_in, pair_irrep, slab_irrep, upper_irrep, virt_irrep):
    core = lax.axis_index("core")
    x1 = lax.axis_index("x1")
    x0 = lax.axis_index("x0")
    slab = lax.axis_index(("z", "y", "core"))
    zy = lax.axis_size("z") * lax.axis_size("y")
    shape = jax.ShapeDtypeStruct
    places = jnp.stack([core, x0, x1, slab])

    other_core, other_x0 = [(0, 1), (1, 0)], [(0, 1), (1, 0)]

    partner = lax.ppermute(integrals, ("x1", "x0"), [(0, 3), (3, 0), (1, 2), (2, 1)])

    steps = 4
    cut = pl.pallas_call(
        functools.partial(cut_body, steps),
        in_specs=[pl.BlockSpec(memory_space=pltpu.HBM)] * 2,
        out_specs=pl.BlockSpec(memory_space=pltpu.HBM),
        out_shape=shape((2 * zy, 8, LANES), BF16),
        scratch_shapes=[
            pltpu.SMEM(pair_irrep.shape, jnp.int32),
            pltpu.VMEM(amplitudes.shape, BF16),
            pltpu.VMEM((2 * zy, 8, LANES), BF16),
            pltpu.SemaphoreType.DMA,
            pltpu.SemaphoreType.DMA((steps,)),
            pltpu.SemaphoreType.DMA((2 * steps,)),
        ],
        cost_estimate=pl.CostEstimate(flops=0, bytes_accessed=700000, transcendentals=0),
    )(pair_irrep, amplitudes)
    cut, block = lax.optimization_barrier((cut, integrals))
    mine = lax.all_to_all(
        cut.reshape(zy, 16, LANES), ("z", "y"), 0, 0, axis_index_groups=[ROLLED], tiled=True
    )
    ab_irrep = jnp.bitwise_xor(upper_irrep[:, None], virt_irrep[None, :])
    kept = (ab_irrep == cut[0, TILES, 0].astype(jnp.int32)).astype(F32)
    kept = jnp.concatenate([kept, jnp.broadcast_to(x1.astype(F32), (1, NV))])
    mine, kept = lax.optimization_barrier((mine, kept))
    mine = mine.reshape(zy, 2, 8, LANES)
    there = lax.ppermute(mine, "x0", other_x0)

    flat, wide = pltpu.VMEM((zy * 8, LANES), F32), pltpu.VMEM((zy, WIDE), F32)
    half, whole = shape((zy, NV), BF16), shape((2 * zy, NV), BF16)
    rows = call(
        functools.partial(rows_body, zy),
        [half, half, shape((zy, NV), F32)],
        "ssvvv",
        24000000 * 300,
        24000000,
        [flat, wide],
    )
    lhs, lhs2, sums = rows(places, slab_irrep, virt_irrep, mine, integrals)
    block2 = lax.ppermute(block, "core", other_core)
    partner, sums = lax.optimization_barrier((partner, sums))
    partner2 = lax.ppermute(partner, "core", other_core)
    after = call(
        functools.partial(there_body, zy),
        [whole, shape((2 * zy * TILES, LANES), F32), shape((2 * zy, NV), F32)],
        "ssvvvvvvvv",
        40000000 * 300,
        40000000,
        [flat, wide, pltpu.VMEM((2 * zy, NV), BF16), pltpu.VMEM((2 * zy, NV), F32)],
    )
    rows2, own_sums, sums = after(
        places, slab_irrep, virt_irrep, there, lhs, lhs2, sums, integrals, block2, partner
    )
    ladder = call(
        functools.partial(ladder_body, zy), shape((2 * zy * 2 * TILES, LANES), F32), "vvvv", 1000, 3000000
    )
    part = ladder(rows2, partner2, sums, own_sums)
    part = (part * SCALE).astype(F16).reshape(2 * zy, TILES, 2, LANES)
    back = lax.all_to_all(
        part, ("x0", "z", "y"), 0, 0, axis_index_groups=[ROLLED + [64 + i for i in ROLLED]], tiled=True
    )
    sums = jnp.sum(back.reshape(2, zy, TILES, 2, LANES).astype(F32), axis=1)
    finish = call(finish_body, shape((1, 4 * NV), BF16), "vvv", 0, 50000)
    return finish(sums, kept, residual_in)


def solution(mesh):
    fine = Mesh(mesh.devices.reshape(8, 8, 2, 2, 2), AXES)
    return jax.shard_map(
        per_device,
        mesh=fine,
        in_specs=(P(AXES, None), P(AXES[:3], AXES[3:]), P(AXES, None), P(AXES), P(), P(), P()),
        out_specs=P(AXES, None),
        check_vma=False,
    )
```

```python
import functools

import jax
import jax.numpy as jnp
from jax import lax
from jax.experimental import pallas as pl
from jax.experimental.pallas import tpu as pltpu
from jax.sharding import Mesh
from jax.sharding import PartitionSpec as P

AXES = ("z", "y", "core", "x1", "x0")
BF16, F32, F16 = jnp.bfloat16, jnp.float32, jnp.float16
NV = 800
LANES = 128
TILES = 7
WIDE = TILES * LANES
ORDER_Z = (5, 6, 7, 0, 1, 2, 3, 4)
ROLLED = [z * 8 + (y + 4) % 8 for z in ORDER_Z for y in range(8)]
SCALE = 64.0

VMEM = pl.BlockSpec(memory_space=pltpu.VMEM)
SMEM = pl.BlockSpec(memory_space=pltpu.SMEM)


def call(body, out, ins, flops, nbytes, scratch=()):
    return pl.pallas_call(
        body,
        out_shape=out,
        in_specs=[SMEM if kind == "s" else VMEM for kind in ins],
        out_specs=jax.tree.map(lambda _: VMEM, out),
        scratch_shapes=list(scratch),
        compiler_params=pltpu.CompilerParams(vmem_limit_bytes=16 * 1024 * 1024),
        cost_estimate=pl.CostEstimate(flops=flops, bytes_accessed=nbytes, transcendentals=0),
    )


def cut_body(steps, pair_ref, row_ref, out_ref, pair, row, cut, pair_sem, in_sems, out_sems):
    lanes, slabs = row.shape[1] // steps, cut.shape[0] // steps
    rows = slabs // 2

    def fetch(i):
        part = pl.ds(i * lanes, lanes)
        return pltpu.make_async_copy(row_ref.at[:, part], row.at[:, part], in_sems.at[i])

    def put(z):
        part = cut.at[pl.ds(z * rows, rows)]
        return pltpu.make_async_copy(part, out_ref.at[pl.ds(ORDER_Z.index(z) * rows, rows)], out_sems.at[z])

    label = pltpu.make_async_copy(pair_ref, pair, pair_sem)
    label.start()

    def four(q, carry):
        for r in range(4):
            at = [pl.multiple_of(q * 3200 + (6 * r + t) * LANES, LANES) for t in range(TILES)]
            tiles = [row[:, pl.ds(a, LANES)].astype(F32) for a in at]
            cut[4 * jnp.bitwise_xor(q, 2) + r] = jnp.concatenate(tiles + [filler], axis=0).astype(BF16)
        return carry

    for i in range(steps):
        fetch(i).start()
    label.wait()
    filler = jnp.full((1, LANES), pair[0].astype(F32))
    for i in range(steps):
        fetch(i).wait()
        lax.fori_loop(i * slabs // 4, (i + 1) * slabs // 4, four, 0, unroll=4)
        put(2 * i).start()
        put(2 * i + 1).start()
    for z in range(2 * steps):
        put(z).wait()


def put_tiles(sums, count, out_ref, first, step):
    wide = jnp.concatenate([sums, jnp.zeros((count, WIDE - NV), F32)], axis=1)
    for t in range(TILES):
        out_ref[pl.ds(first + t, count, stride=step), :] = wide[:, t * LANES : (t + 1) * LANES]


def kept_rows(flip, zy, places_ref, slab_ref, virt_ref, tiles_ref, flat, wide, lhs_ref, first):
    c = jnp.bitwise_xor(places_ref[3], flip)
    flat[...] = tiles_ref[:, jnp.bitwise_xor(places_ref[0], flip)].astype(F32).reshape(zy * 8, LANES)
    for t in range(TILES):
        wide[:, t * LANES : (t + 1) * LANES] = flat[pl.ds(t, zy, stride=8), :]
    pair = flat[pl.ds(TILES, zy, stride=8), :][:, 0:1]
    cd = jnp.bitwise_xor(virt_ref[...].reshape(1, NV), slab_ref[c]).astype(F32)
    for shift in range(4):

        @pl.when(c % 4 == shift)
        def _():
            row = wide[:, 32 * shift : 32 * shift + NV]
            lhs_ref[pl.ds(first, zy), :] = jnp.where(pair == cd, row, 0.0).astype(BF16)


def rows_body(zy, places_ref, slab_ref, virt_ref, tiles_ref, own_ref, lhs_ref, lhs2_ref, out_ref, flat, wide):
    kept_rows(0, zy, places_ref, slab_ref, virt_ref, tiles_ref, flat, wide, lhs_ref, 0)
    out_ref[...] = jnp.dot(lhs_ref[...], own_ref[...], preferred_element_type=F32)
    kept_rows(1, zy, places_ref, slab_ref, virt_ref, tiles_ref, flat, wide, lhs2_ref, 0)


def there_body(zy, *refs):
    places_ref, slab_ref, virt_ref, tiles_ref, lhs_ref, lhs2_ref, sums_ref = refs[:7]
    own_ref, own2_ref, block_ref = refs[7:10]
    rows2_ref, own_sums_ref, out_ref, flat, wide, rows, sums = refs[10:]
    here = pl.multiple_of(places_ref[1] * zy, zy)
    there = pl.multiple_of(zy - here, zy)
    rows[pl.ds(here, zy), :] = lhs_ref[...]
    rows2_ref[pl.ds(here, zy), :] = lhs2_ref[...]
    sums[pl.ds(here, zy), :] = sums_ref[...]
    kept_rows(0, zy, places_ref, slab_ref, virt_ref, tiles_ref, flat, wide, rows, there)
    kept_rows(1, zy, places_ref, slab_ref, virt_ref, tiles_ref, flat, wide, rows2_ref, there)
    own = jnp.dot(rows[pl.ds(there, zy), :], own_ref[...], preferred_element_type=F32)
    sums[pl.ds(there, zy), :] = own
    own = sums[...] + jnp.dot(rows2_ref[...], own2_ref[...], preferred_element_type=F32)
    put_tiles(own, 2 * zy, own_sums_ref, 0, TILES)
    out_ref[...] = jnp.dot(rows[...], block_ref[...], preferred_element_type=F32)


def ladder_body(zy, lhs_ref, block_ref, sums_ref, own_ref, out_ref):
    sums = sums_ref[...] + jnp.dot(lhs_ref[...], block_ref[...], preferred_element_type=F32)
    put_tiles(sums, 2 * zy, out_ref, TILES, 2 * TILES)
    for t in range(TILES):
        out_ref[pl.ds(t, 2 * zy, stride=2 * TILES), :] = own_ref[pl.ds(t, 2 * zy, stride=TILES), :]


def finish_body(sums_ref, kept_ref, old_ref, out_ref):
    swap = kept_ref[4:5, 0:LANES] > 0.5
    order = ((0, 0), (1, 0), (1, 1), (0, 1))
    for a in range(4):
        (s, h), (s2, h2) = order[a], order[(a + 2) % 4]
        tiles = []
        for t in range(TILES):
            (p, q), (p2, q2) = divmod(TILES * h + t, 2), divmod(TILES * h2 + t, 2)
            tiles.append(jnp.where(swap, sums_ref[s2, p2, q2 : q2 + 1, :], sums_ref[s, p, q : q + 1, :]))
        row = jnp.concatenate(tiles, axis=1)[:, :NV] * (1.0 / SCALE)
        row = jnp.where(kept_ref[a : a + 1, :] > 0.5, row, 0.0)
        old = old_ref[:, a * NV : (a + 1) * NV].astype(F32)
        out_ref[:, a * NV : (a + 1) * NV] = (old + row).astype(BF16)


def per_device(amplitudes, integrals, residual_in, pair_irrep, slab_irrep, upper_irrep, virt_irrep):
    core = lax.axis_index("core")
    x1 = lax.axis_index("x1")
    x0 = lax.axis_index("x0")
    slab = lax.axis_index(("z", "y", "core"))
    zy = lax.axis_size("z") * lax.axis_size("y")
    shape = jax.ShapeDtypeStruct
    places = jnp.stack([core, x0, x1, slab])

    other_core, other_x0 = [(0, 1), (1, 0)], [(0, 1), (1, 0)]

    partner = lax.ppermute(integrals, ("x1", "x0"), [(0, 3), (3, 0), (1, 2), (2, 1)])

    steps = 4
    cut = pl.pallas_call(
        functools.partial(cut_body, steps),
        in_specs=[pl.BlockSpec(memory_space=pltpu.HBM)] * 2,
        out_specs=pl.BlockSpec(memory_space=pltpu.HBM),
        out_shape=shape((2 * zy, 8, LANES), BF16),
        scratch_shapes=[
            pltpu.SMEM(pair_irrep.shape, jnp.int32),
            pltpu.VMEM(amplitudes.shape, BF16),
            pltpu.VMEM((2 * zy, 8, LANES), BF16),
            pltpu.SemaphoreType.DMA,
            pltpu.SemaphoreType.DMA((steps,)),
            pltpu.SemaphoreType.DMA((2 * steps,)),
        ],
        cost_estimate=pl.CostEstimate(flops=0, bytes_accessed=700000, transcendentals=0),
    )(pair_irrep, amplitudes)
    cut, block = lax.optimization_barrier((cut, integrals))
    mine = lax.all_to_all(
        cut.reshape(zy, 16, LANES), ("z", "y"), 0, 0, axis_index_groups=[ROLLED], tiled=True
    )
    ab_irrep = jnp.bitwise_xor(upper_irrep[:, None], virt_irrep[None, :])
    kept = (ab_irrep == cut[0, TILES, 0].astype(jnp.int32)).astype(F32)
    kept = jnp.concatenate([kept, jnp.broadcast_to(x1.astype(F32), (1, NV))])
    mine, kept = lax.optimization_barrier((mine, kept))
    mine = mine.reshape(zy, 2, 8, LANES)
    there = lax.ppermute(mine, "x0", other_x0)

    flat, wide = pltpu.VMEM((zy * 8, LANES), F32), pltpu.VMEM((zy, WIDE), F32)
    half, whole = shape((zy, NV), BF16), shape((2 * zy, NV), BF16)
    rows = call(
        functools.partial(rows_body, zy),
        [half, half, shape((zy, NV), F32)],
        "ssvvv",
        24000000 * 300,
        24000000,
        [flat, wide],
    )
    lhs, lhs2, sums = rows(places, slab_irrep, virt_irrep, mine, integrals)
    block2 = lax.ppermute(block, "core", other_core)
    partner, sums = lax.optimization_barrier((partner, sums))
    partner2 = lax.ppermute(partner, "core", other_core)
    after = call(
        functools.partial(there_body, zy),
        [whole, shape((2 * zy * TILES, LANES), F32), shape((2 * zy, NV), F32)],
        "ssvvvvvvvv",
        40000000 * 300,
        40000000,
        [flat, wide, pltpu.VMEM((2 * zy, NV), BF16), pltpu.VMEM((2 * zy, NV), F32)],
    )
    rows2, own_sums, sums = after(
        places, slab_irrep, virt_irrep, there, lhs, lhs2, sums, integrals, block2, partner
    )
    ladder = call(
        functools.partial(ladder_body, zy), shape((2 * zy * 2 * TILES, LANES), F32), "vvvv", 1000, 3000000
    )
    part = ladder(rows2, partner2, sums, own_sums)
    part = (part * SCALE).astype(F16).reshape(2 * zy, TILES, 2, LANES)
    back = lax.all_to_all(
        part, ("x0", "z", "y"), 0, 0, axis_index_groups=[ROLLED + [64 + i for i in ROLLED]], tiled=True
    )
    sums = jnp.sum(back.reshape(2, zy, TILES, 2, LANES).astype(F32), axis=1)
    finish = call(finish_body, shape((1, 4 * NV), BF16), "vvv", 0, 50000)
    return finish(sums, kept, residual_in)


def solution(mesh):
    fine = Mesh(mesh.devices.reshape(8, 8, 2, 2, 2), AXES)
    return jax.shard_map(
        per_device,
        mesh=fine,
        in_specs=(P(AXES, None), P(AXES[:3], AXES[3:]), P(AXES, None), P(AXES), P(), P(), P()),
        out_specs=P(AXES, None),
        check_vma=False,
    )
```

```python
import functools

import jax
import jax.numpy as jnp
from jax import lax
from jax.experimental import pallas as pl
from jax.experimental.pallas import tpu as pltpu
from jax.sharding import Mesh
from jax.sharding import PartitionSpec as P

AXES = ("z", "y", "core", "x1", "x0")
BF16, F32, F16 = jnp.bfloat16, jnp.float32, jnp.float16
NV = 800
LANES = 128
TILES = 7
WIDE = TILES * LANES
ORDER_Z = (5, 6, 7, 0, 1, 2, 3, 4)
ROLLED = [z * 8 + (y + 4) % 8 for z in ORDER_Z for y in range(8)]
SCALE = 64.0

VMEM = pl.BlockSpec(memory_space=pltpu.VMEM)
SMEM = pl.BlockSpec(memory_space=pltpu.SMEM)


def call(body, out, ins, flops, nbytes, scratch=()):
    return pl.pallas_call(
        body,
        out_shape=out,
        in_specs=[SMEM if kind == "s" else VMEM for kind in ins],
        out_specs=jax.tree.map(lambda _: VMEM, out),
        scratch_shapes=list(scratch),
        compiler_params=pltpu.CompilerParams(vmem_limit_bytes=16 * 1024 * 1024),
        cost_estimate=pl.CostEstimate(flops=flops, bytes_accessed=nbytes, transcendentals=0),
    )


def cut_body(steps, pair_ref, row_ref, out_ref, pair, row, cut, pair_sem, in_sems, out_sems):
    lanes, slabs = row.shape[1] // steps, cut.shape[0] // steps
    rows = slabs // 2

    def fetch(i):
        part = pl.ds(i * lanes, lanes)
        return pltpu.make_async_copy(row_ref.at[:, part], row.at[:, part], in_sems.at[i])

    def put(z):
        part = cut.at[pl.ds(z * rows, rows)]
        return pltpu.make_async_copy(part, out_ref.at[pl.ds(ORDER_Z.index(z) * rows, rows)], out_sems.at[z])

    label = pltpu.make_async_copy(pair_ref, pair, pair_sem)
    label.start()

    def four(q, carry):
        for r in range(4):
            at = [pl.multiple_of(q * 3200 + (6 * r + t) * LANES, LANES) for t in range(TILES)]
            tiles = [row[:, pl.ds(a, LANES)].astype(F32) for a in at]
            cut[4 * jnp.bitwise_xor(q, 2) + r] = jnp.concatenate(tiles + [filler], axis=0).astype(BF16)
        return carry

    for i in range(steps):
        fetch(i).start()
    label.wait()
    filler = jnp.full((1, LANES), pair[0].astype(F32))
    for i in range(steps):
        fetch(i).wait()
        lax.fori_loop(i * slabs // 4, (i + 1) * slabs // 4, four, 0, unroll=4)
        put(2 * i).start()
        put(2 * i + 1).start()
    for z in range(2 * steps):
        put(z).wait()


def put_tiles(sums, count, out_ref, first, step):
    wide = jnp.concatenate([sums, jnp.zeros((count, WIDE - NV), F32)], axis=1)
    for t in range(TILES):
        out_ref[pl.ds(first + t, count, stride=step), :] = wide[:, t * LANES : (t + 1) * LANES]


def kept_rows(flip, zy, places_ref, slab_ref, virt_ref, tiles_ref, flat, wide, lhs_ref, first):
    c = jnp.bitwise_xor(places_ref[3], flip)
    flat[...] = tiles_ref[:, jnp.bitwise_xor(places_ref[0], flip)].astype(F32).reshape(zy * 8, LANES)
    for t in range(TILES):
        wide[:, t * LANES : (t + 1) * LANES] = flat[pl.ds(t, zy, stride=8), :]
    pair = flat[pl.ds(TILES, zy, stride=8), :][:, 0:1]
    cd = jnp.bitwise_xor(virt_ref[...].reshape(1, NV), slab_ref[c]).astype(F32)
    for shift in range(4):

        @pl.when(c % 4 == shift)
        def _():
            row = wide[:, 32 * shift : 32 * shift + NV]
            lhs_ref[pl.ds(first, zy), :] = jnp.where(pair == cd, row, 0.0).astype(BF16)


def rows_body(zy, places_ref, slab_ref, virt_ref, tiles_ref, own_ref, lhs_ref, lhs2_ref, out_ref, flat, wide):
    kept_rows(0, zy, places_ref, slab_ref, virt_ref, tiles_ref, flat, wide, lhs_ref, 0)
    out_ref[...] = jnp.dot(lhs_ref[...], own_ref[...], preferred_element_type=F32)
    kept_rows(1, zy, places_ref, slab_ref, virt_ref, tiles_ref, flat, wide, lhs2_ref, 0)


def there_body(zy, *refs):
    places_ref, slab_ref, virt_ref, tiles_ref, lhs_ref, lhs2_ref, sums_ref = refs[:7]
    own_ref, own2_ref, block_ref = refs[7:10]
    rows2_ref, own_sums_ref, out_ref, flat, wide, rows, sums = refs[10:]
    here = pl.multiple_of((1 - places_ref[1]) * zy, zy)
    there = pl.multiple_of(zy - here, zy)
    rows[pl.ds(here, zy), :] = lhs_ref[...]
    rows2_ref[pl.ds(here, zy), :] = lhs2_ref[...]
    sums[pl.ds(here, zy), :] = sums_ref[...]
    kept_rows(0, zy, places_ref, slab_ref, virt_ref, tiles_ref, flat, wide, rows, there)
    kept_rows(1, zy, places_ref, slab_ref, virt_ref, tiles_ref, flat, wide, rows2_ref, there)
    own = jnp.dot(rows[pl.ds(there, zy), :], own_ref[...], preferred_element_type=F32)
    sums[pl.ds(there, zy), :] = own
    own = sums[...] + jnp.dot(rows2_ref[...], own2_ref[...], preferred_element_type=F32)
    put_tiles(own, 2 * zy, own_sums_ref, 0, TILES)
    out_ref[...] = jnp.dot(rows[...], block_ref[...], preferred_element_type=F32)


def ladder_body(zy, lhs_ref, block_ref, sums_ref, own_ref, out_ref):
    sums = sums_ref[...] + jnp.dot(lhs_ref[...], block_ref[...], preferred_element_type=F32)
    put_tiles(sums, 2 * zy, out_ref, TILES, 2 * TILES)
    for t in range(TILES):
        out_ref[pl.ds(t, 2 * zy, stride=2 * TILES), :] = own_ref[pl.ds(t, 2 * zy, stride=TILES), :]


def finish_body(sums_ref, kept_ref, old_ref, out_ref):
    swap = kept_ref[4:5, 0:LANES] > 0.5
    order = ((1, 0), (0, 0), (0, 1), (1, 1))
    for a in range(4):
        (s, h), (s2, h2) = order[a], order[(a + 2) % 4]
        tiles = []
        for t in range(TILES):
            (p, q), (p2, q2) = divmod(TILES * h + t, 2), divmod(TILES * h2 + t, 2)
            tiles.append(jnp.where(swap, sums_ref[s2, p2, q2 : q2 + 1, :], sums_ref[s, p, q : q + 1, :]))
        row = jnp.concatenate(tiles, axis=1)[:, :NV] * (1.0 / SCALE)
        row = jnp.where(kept_ref[a : a + 1, :] > 0.5, row, 0.0)
        old = old_ref[:, a * NV : (a + 1) * NV].astype(F32)
        out_ref[:, a * NV : (a + 1) * NV] = (old + row).astype(BF16)


def per_device(amplitudes, integrals, residual_in, pair_irrep, slab_irrep, upper_irrep, virt_irrep):
    core = lax.axis_index("core")
    x1 = lax.axis_index("x1")
    x0 = lax.axis_index("x0")
    slab = lax.axis_index(("z", "y", "core"))
    zy = lax.axis_size("z") * lax.axis_size("y")
    shape = jax.ShapeDtypeStruct
    places = jnp.stack([core, x0, x1, slab])

    other_core, other_x0 = [(0, 1), (1, 0)], [(0, 1), (1, 0)]

    partner = lax.ppermute(integrals, ("x1", "x0"), [(0, 3), (3, 0), (1, 2), (2, 1)])

    steps = 4
    cut = pl.pallas_call(
        functools.partial(cut_body, steps),
        in_specs=[pl.BlockSpec(memory_space=pltpu.HBM)] * 2,
        out_specs=pl.BlockSpec(memory_space=pltpu.HBM),
        out_shape=shape((2 * zy, 8, LANES), BF16),
        scratch_shapes=[
            pltpu.SMEM(pair_irrep.shape, jnp.int32),
            pltpu.VMEM(amplitudes.shape, BF16),
            pltpu.VMEM((2 * zy, 8, LANES), BF16),
            pltpu.SemaphoreType.DMA,
            pltpu.SemaphoreType.DMA((steps,)),
            pltpu.SemaphoreType.DMA((2 * steps,)),
        ],
        cost_estimate=pl.CostEstimate(flops=0, bytes_accessed=700000, transcendentals=0),
    )(pair_irrep, amplitudes)
    cut, block = lax.optimization_barrier((cut, integrals))
    mine = lax.all_to_all(
        cut.reshape(zy, 16, LANES), ("z", "y"), 0, 0, axis_index_groups=[ROLLED], tiled=True
    )
    ab_irrep = jnp.bitwise_xor(upper_irrep[:, None], virt_irrep[None, :])
    kept = (ab_irrep == cut[0, TILES, 0].astype(jnp.int32)).astype(F32)
    kept = jnp.concatenate([kept, jnp.broadcast_to(x1.astype(F32), (1, NV))])
    mine, kept = lax.optimization_barrier((mine, kept))
    mine = mine.reshape(zy, 2, 8, LANES)
    there = lax.ppermute(mine, "x0", other_x0)

    flat, wide = pltpu.VMEM((zy * 8, LANES), F32), pltpu.VMEM((zy, WIDE), F32)
    half, whole = shape((zy, NV), BF16), shape((2 * zy, NV), BF16)
    rows = call(
        functools.partial(rows_body, zy),
        [half, half, shape((zy, NV), F32)],
        "ssvvv",
        24000000 * 300,
        24000000,
        [flat, wide],
    )
    lhs, lhs2, sums = rows(places, slab_irrep, virt_irrep, mine, integrals)
    block2 = lax.ppermute(block, "core", other_core)
    partner, sums = lax.optimization_barrier((partner, sums))
    partner2 = lax.ppermute(partner, "core", other_core)
    after = call(
        functools.partial(there_body, zy),
        [whole, shape((2 * zy * TILES, LANES), F32), shape((2 * zy, NV), F32)],
        "ssvvvvvvvv",
        40000000 * 300,
        40000000,
        [flat, wide, pltpu.VMEM((2 * zy, NV), BF16), pltpu.VMEM((2 * zy, NV), F32)],
    )
    rows2, own_sums, sums = after(
        places, slab_irrep, virt_irrep, there, lhs, lhs2, sums, integrals, block2, partner
    )
    ladder = call(
        functools.partial(ladder_body, zy), shape((2 * zy * 2 * TILES, LANES), F32), "vvvv", 1000, 3000000
    )
    part = ladder(rows2, partner2, sums, own_sums)
    part = (part * SCALE).astype(F16).reshape(2 * zy, TILES, 2, LANES)
    back = lax.all_to_all(
        part, ("x0", "z", "y"), 0, 0, axis_index_groups=[[64 + i for i in ROLLED] + ROLLED], tiled=True
    )
    sums = jnp.sum(back.reshape(2, zy, TILES, 2, LANES).astype(F32), axis=1)
    finish = call(finish_body, shape((1, 4 * NV), BF16), "vvv", 0, 50000)
    return finish(sums, kept, residual_in)


def solution(mesh):
    fine = Mesh(mesh.devices.reshape(8, 8, 2, 2, 2), AXES)
    return jax.shard_map(
        per_device,
        mesh=fine,
        in_specs=(P(AXES, None), P(AXES[:3], AXES[3:]), P(AXES, None), P(AXES), P(), P(), P()),
        out_specs=P(AXES, None),
        check_vma=False,
    )
```

```python
import functools

import jax
import jax.numpy as jnp
from jax import lax
from jax.experimental import pallas as pl
from jax.experimental.pallas import tpu as pltpu
from jax.sharding import Mesh
from jax.sharding import PartitionSpec as P

AXES = ("z", "y", "core", "x1", "x0")
BF16, F32, F16 = jnp.bfloat16, jnp.float32, jnp.float16
NV = 800
LANES = 128
TILES = 7
WIDE = TILES * LANES
ORDER_Z = (4, 5, 6, 7, 0, 1, 2, 3)
ROLLED = [z * 8 + (y + 4) % 8 for z in ORDER_Z for y in range(8)]
SCALE = 64.0

VMEM = pl.BlockSpec(memory_space=pltpu.VMEM)
SMEM = pl.BlockSpec(memory_space=pltpu.SMEM)


def call(body, out, ins, flops, nbytes, scratch=()):
    return pl.pallas_call(
        body,
        out_shape=out,
        in_specs=[SMEM if kind == "s" else VMEM for kind in ins],
        out_specs=jax.tree.map(lambda _: VMEM, out),
        scratch_shapes=list(scratch),
        compiler_params=pltpu.CompilerParams(vmem_limit_bytes=16 * 1024 * 1024),
        cost_estimate=pl.CostEstimate(flops=flops, bytes_accessed=nbytes, transcendentals=0),
    )


def cut_body(steps, pair_ref, row_ref, out_ref, pair, row, cut, pair_sem, in_sems, out_sems):
    lanes, slabs = row.shape[1] // steps, cut.shape[0] // steps
    rows = slabs // 2

    def fetch(i):
        part = pl.ds(i * lanes, lanes)
        return pltpu.make_async_copy(row_ref.at[:, part], row.at[:, part], in_sems.at[i])

    def put(z):
        part = cut.at[pl.ds(z * rows, rows)]
        return pltpu.make_async_copy(part, out_ref.at[pl.ds(ORDER_Z.index(z) * rows, rows)], out_sems.at[z])

    label = pltpu.make_async_copy(pair_ref, pair, pair_sem)
    label.start()

    def four(q, carry):
        for r in range(4):
            at = [pl.multiple_of(q * 3200 + (6 * r + t) * LANES, LANES) for t in range(TILES)]
            tiles = [row[:, pl.ds(a, LANES)].astype(F32) for a in at]
            cut[4 * jnp.bitwise_xor(q, 2) + r] = jnp.concatenate(tiles + [filler], axis=0).astype(BF16)
        return carry

    for i in range(steps):
        fetch(i).start()
    label.wait()
    filler = jnp.full((1, LANES), pair[0].astype(F32))
    for i in range(steps):
        fetch(i).wait()
        lax.fori_loop(i * slabs // 4, (i + 1) * slabs // 4, four, 0, unroll=4)
        put(2 * i).start()
        put(2 * i + 1).start()
    for z in range(2 * steps):
        put(z).wait()


def put_tiles(sums, count, out_ref, first, step):
    wide = jnp.concatenate([sums, jnp.zeros((count, WIDE - NV), F32)], axis=1)
    for t in range(TILES):
        out_ref[pl.ds(first + t, count, stride=step), :] = wide[:, t * LANES : (t + 1) * LANES]


def kept_rows(flip, zy, places_ref, slab_ref, virt_ref, tiles_ref, flat, wide, lhs_ref, first):
    c = jnp.bitwise_xor(places_ref[3], flip)
    flat[...] = tiles_ref[:, jnp.bitwise_xor(places_ref[0], flip)].astype(F32).reshape(zy * 8, LANES)
    for t in range(TILES):
        wide[:, t * LANES : (t + 1) * LANES] = flat[pl.ds(t, zy, stride=8), :]
    pair = flat[pl.ds(TILES, zy, stride=8), :][:, 0:1]
    cd = jnp.bitwise_xor(virt_ref[...].reshape(1, NV), slab_ref[c]).astype(F32)
    for shift in range(4):

        @pl.when(c % 4 == shift)
        def _():
            row = wide[:, 32 * shift : 32 * shift + NV]
            lhs_ref[pl.ds(first, zy), :] = jnp.where(pair == cd, row, 0.0).astype(BF16)


def rows_body(zy, places_ref, slab_ref, virt_ref, tiles_ref, own_ref, lhs_ref, lhs2_ref, out_ref, flat, wide):
    kept_rows(0, zy, places_ref, slab_ref, virt_ref, tiles_ref, flat, wide, lhs_ref, 0)
    out_ref[...] = jnp.dot(lhs_ref[...], own_ref[...], preferred_element_type=F32)
    kept_rows(1, zy, places_ref, slab_ref, virt_ref, tiles_ref, flat, wide, lhs2_ref, 0)


def there_body(zy, *refs):
    places_ref, slab_ref, virt_ref, tiles_ref, lhs_ref, lhs2_ref, sums_ref = refs[:7]
    own_ref, own2_ref, block_ref = refs[7:10]
    rows2_ref, own_sums_ref, out_ref, flat, wide, rows, sums = refs[10:]
    here = pl.multiple_of((1 - places_ref[1]) * zy, zy)
    there = pl.multiple_of(zy - here, zy)
    rows[pl.ds(here, zy), :] = lhs_ref[...]
    rows2_ref[pl.ds(here, zy), :] = lhs2_ref[...]
    sums[pl.ds(here, zy), :] = sums_ref[...]
    kept_rows(0, zy, places_ref, slab_ref, virt_ref, tiles_ref, flat, wide, rows, there)
    kept_rows(1, zy, places_ref, slab_ref, virt_ref, tiles_ref, flat, wide, rows2_ref, there)
    own = jnp.dot(rows[pl.ds(there, zy), :], own_ref[...], preferred_element_type=F32)
    sums[pl.ds(there, zy), :] = own
    own = sums[...] + jnp.dot(rows2_ref[...], own2_ref[...], preferred_element_type=F32)
    put_tiles(own, 2 * zy, own_sums_ref, 0, TILES)
    out_ref[...] = jnp.dot(rows[...], block_ref[...], preferred_element_type=F32)


def ladder_body(zy, lhs_ref, block_ref, sums_ref, own_ref, out_ref):
    sums = sums_ref[...] + jnp.dot(lhs_ref[...], block_ref[...], preferred_element_type=F32)
    put_tiles(sums, 2 * zy, out_ref, TILES, 2 * TILES)
    for t in range(TILES):
        out_ref[pl.ds(t, 2 * zy, stride=2 * TILES), :] = own_ref[pl.ds(t, 2 * zy, stride=TILES), :]


def finish_body(sums_ref, kept_ref, old_ref, out_ref):
    swap = kept_ref[4:5, 0:LANES] > 0.5
    order = ((1, 0), (0, 0), (0, 1), (1, 1))
    for a in range(4):
        (s, h), (s2, h2) = order[a], order[(a + 2) % 4]
        tiles = []
        for t in range(TILES):
            (p, q), (p2, q2) = divmod(TILES * h + t, 2), divmod(TILES * h2 + t, 2)
            tiles.append(jnp.where(swap, sums_ref[s2, p2, q2 : q2 + 1, :], sums_ref[s, p, q : q + 1, :]))
        row = jnp.concatenate(tiles, axis=1)[:, :NV] * (1.0 / SCALE)
        row = jnp.where(kept_ref[a : a + 1, :] > 0.5, row, 0.0)
        old = old_ref[:, a * NV : (a + 1) * NV].astype(F32)
        out_ref[:, a * NV : (a + 1) * NV] = (old + row).astype(BF16)


def per_device(amplitudes, integrals, residual_in, pair_irrep, slab_irrep, upper_irrep, virt_irrep):
    core = lax.axis_index("core")
    x1 = lax.axis_index("x1")
    x0 = lax.axis_index("x0")
    slab = lax.axis_index(("z", "y", "core"))
    zy = lax.axis_size("z") * lax.axis_size("y")
    shape = jax.ShapeDtypeStruct
    places = jnp.stack([core, x0, x1, slab])

    other_core, other_x0 = [(0, 1), (1, 0)], [(0, 1), (1, 0)]

    partner = lax.ppermute(integrals, ("x1", "x0"), [(0, 3), (3, 0), (1, 2), (2, 1)])

    steps = 4
    cut = pl.pallas_call(
        functools.partial(cut_body, steps),
        in_specs=[pl.BlockSpec(memory_space=pltpu.HBM)] * 2,
        out_specs=pl.BlockSpec(memory_space=pltpu.HBM),
        out_shape=shape((2 * zy, 8, LANES), BF16),
        scratch_shapes=[
            pltpu.SMEM(pair_irrep.shape, jnp.int32),
            pltpu.VMEM(amplitudes.shape, BF16),
            pltpu.VMEM((2 * zy, 8, LANES), BF16),
            pltpu.SemaphoreType.DMA,
            pltpu.SemaphoreType.DMA((steps,)),
            pltpu.SemaphoreType.DMA((2 * steps,)),
        ],
        cost_estimate=pl.CostEstimate(flops=0, bytes_accessed=700000, transcendentals=0),
    )(pair_irrep, amplitudes)
    cut, block = lax.optimization_barrier((cut, integrals))
    mine = lax.all_to_all(
        cut.reshape(zy, 16, LANES), ("z", "y"), 0, 0, axis_index_groups=[ROLLED], tiled=True
    )
    ab_irrep = jnp.bitwise_xor(upper_irrep[:, None], virt_irrep[None, :])
    kept = (ab_irrep == cut[0, TILES, 0].astype(jnp.int32)).astype(F32)
    kept = jnp.concatenate([kept, jnp.broadcast_to(x1.astype(F32), (1, NV))])
    mine, kept = lax.optimization_barrier((mine, kept))
    mine = mine.reshape(zy, 2, 8, LANES)
    there = lax.ppermute(mine, "x0", other_x0)

    flat, wide = pltpu.VMEM((zy * 8, LANES), F32), pltpu.VMEM((zy, WIDE), F32)
    half, whole = shape((zy, NV), BF16), shape((2 * zy, NV), BF16)
    rows = call(
        functools.partial(rows_body, zy),
        [half, half, shape((zy, NV), F32)],
        "ssvvv",
        24000000 * 300,
        24000000,
        [flat, wide],
    )
    lhs, lhs2, sums = rows(places, slab_irrep, virt_irrep, mine, integrals)
    block2 = lax.ppermute(block, "core", other_core)
    partner, sums = lax.optimization_barrier((partner, sums))
    partner2 = lax.ppermute(partner, "core", other_core)
    after = call(
        functools.partial(there_body, zy),
        [whole, shape((2 * zy * TILES, LANES), F32), shape((2 * zy, NV), F32)],
        "ssvvvvvvvv",
        40000000 * 300,
        40000000,
        [flat, wide, pltpu.VMEM((2 * zy, NV), BF16), pltpu.VMEM((2 * zy, NV), F32)],
    )
    rows2, own_sums, sums = after(
        places, slab_irrep, virt_irrep, there, lhs, lhs2, sums, integrals, block2, partner
    )
    ladder = call(
        functools.partial(ladder_body, zy), shape((2 * zy * 2 * TILES, LANES), F32), "vvvv", 1000, 3000000
    )
    part = ladder(rows2, partner2, sums, own_sums)
    part = (part * SCALE).astype(F16).reshape(2 * zy, TILES, 2, LANES)
    back = lax.all_to_all(
        part, ("x0", "z", "y"), 0, 0, axis_index_groups=[[64 + i for i in ROLLED] + ROLLED], tiled=True
    )
    sums = jnp.sum(back.reshape(2, zy, TILES, 2, LANES).astype(F32), axis=1)
    finish = call(finish_body, shape((1, 4 * NV), BF16), "vvv", 0, 50000)
    return finish(sums, kept, residual_in)


def solution(mesh):
    fine = Mesh(mesh.devices.reshape(8, 8, 2, 2, 2), AXES)
    return jax.shard_map(
        per_device,
        mesh=fine,
        in_specs=(P(AXES, None), P(AXES[:3], AXES[3:]), P(AXES, None), P(AXES), P(), P(), P()),
        out_specs=P(AXES, None),
        check_vma=False,
    )
```
